32 devices in a mesh: dp: 4 (over y, core), tensor: 8 (over z, x).
Axes of the slice: x: 2, y: 2, z: 4, core: 2. Of those that a mesh axis runs over, the one named last changes fastest.
Arguments:
- hidden: bfloat16 [640, 16384], P(None, ('dp', 'tensor')), may hold values from -100 to 100
- gain: bfloat16 [1, 16384], P(None, ('dp', 'tensor')), may hold values from 0.5 to 2, as said below
- head_weight: bfloat16 [16384, 65536], P('dp', 'tensor'), may hold values from -3 to 3
- draft_probs: float32 [640, 65536], P(('dp', 'tensor')), may hold values from 0 to 1, as said below
- draft_ids: int32 [640], P('dp'), may hold values from 0 to 65535
- reject_at: int32 [128], P('dp'), may hold values from 0 to 4
Outputs:
- token_logprob: float32 [640], P('dp')
- residual: float32 [128, 65536], P('dp', 'tensor')
The draws below stay inside these ranges and needn't reach their ends.
Inputs may be any that keep to these rules, and one draw needn't show every extreme that they name: `draft_probs`: every row is a probability distribution over the 65536 entries that sums to one. `gain`: positive.
All inputs are finite; a program needn't handle non-finite values.
Results may differ from the reference program's by a relative error of at most 0.0005.
The reference program's roundings to bfloat16 on the way (of `normed`) count: a program that leaves them out, or rounds other values in their place, can miss the bound.
Values may be sent and summed in bfloat16 or wider, within the bound.
No kernel may reach another device: no remote copies, remote signals or barrier semaphores. Data moves between devices by JAX's collectives and lax.ppermute only.
A program may use at most 192 MiB of HBM per device.

```python
import jax
import jax.numpy as jnp
from jax import lax

D = 16384
VOCAB = 65536
POS = 5
ROWS = 128
TOKENS = 640
N_DP = 4


def shared_direction(key, which):
    inner = jax.random.fold_in(key, 501 + which)
    flips = jax.random.bernoulli(inner, 0.5, (D,))
    return jnp.where(flips, 1.0, -1.0).astype(jnp.float32)


def draw_hidden(key, part):
    first, second = jax.random.split(jax.random.fold_in(key, 11), 2)
    ramp = jnp.exp(jnp.log(3.0) * jnp.arange(D, dtype=jnp.float32) / D)
    rough = jax.random.uniform(second, (D,), jnp.float32, 0.5, 1.5)
    base = jnp.clip(jax.random.normal(first, (TOKENS, D), jnp.float32), -5.0, 5.0)
    drawn = base * ramp * rough
    noise = jax.random.uniform(jax.random.fold_in(key, 13), (TOKENS, D), jnp.float32, -0.05, 0.05)
    slot = jnp.arange(TOKENS) % 16
    along_first = shared_direction(key, 0)[None, :] + noise
    along_second = shared_direction(key, 1)[None, :] + noise
    mixed = jnp.where((slot == 3)[:, None], along_first, drawn)
    mixed = jnp.where((slot == 11)[:, None], along_second, mixed)
    return mixed.astype(jnp.bfloat16)


def draw_gain(key, part):
    inner = jax.random.fold_in(key, 23)
    return jnp.clip(1.0 + 0.1 * jax.random.normal(inner, (1, D), jnp.float32), 0.5, 1.5).astype(jnp.bfloat16)


def draw_head_weight(key, part):
    inner = jax.random.fold_in(key, 29)
    base = jnp.clip(jax.random.normal(inner, (D, VOCAB), jnp.float32), -5.0, 5.0) * (9.0 / D) ** 0.5
    quarter = VOCAB // 4
    offsets = jax.random.randint(jax.random.fold_in(key, 601), (4,), 0, quarter)
    places = jnp.arange(4, dtype=jnp.int32) * quarter + offsets
    first = shared_direction(key, 0)
    second = shared_direction(key, 1)
    added = jnp.stack([120.0 * first, 118.0 * first, 230.0 * second, 228.0 * second], axis=1) / D
    return base.at[:, places].add(added).astype(jnp.bfloat16)


def draw_draft_probs(key, part):
    inner = jax.random.fold_in(key, 37)
    scores = 3.0 * jax.random.normal(inner, (TOKENS, VOCAB), jnp.float32)
    return jax.nn.softmax(scores, axis=1)


def set_ends(values, own_key, least, largest):
    longest = values.shape.index(max(values.shape))
    spots = []
    for shift in (0, 1):
        where = [jax.random.randint(jax.random.fold_in(own_key, axis), (), 0, length) for axis, length in enumerate(values.shape)]
        where[longest] = (where[longest] + shift) % values.shape[longest]
        spots.append(tuple(where))
    return values.at[spots[0]].set(least).at[spots[1]].set(largest)


def setup_inputs(seed: int = 0) -> dict:
    keys = jax.random.split(jax.random.key(seed), 7)
    hidden = draw_hidden(jax.random.fold_in(keys[6], 71), 0)
    gain = draw_gain(jax.random.fold_in(keys[6], 71), 0)
    head_weight = draw_head_weight(jax.random.fold_in(keys[6], 71), 0)
    draft_probs = draw_draft_probs(jax.random.fold_in(keys[6], 71), 0)
    draft_ids = set_ends(jax.random.randint(keys[4], (TOKENS,), 0, VOCAB), jax.random.fold_in(keys[4], 1), 0, VOCAB - 1).astype(jnp.int32)
    reject_at = set_ends(jax.random.randint(keys[5], (ROWS,), 0, POS), jax.random.fold_in(keys[5], 1), 0, POS - 1).astype(jnp.int32)
    return {"hidden": hidden, "gain": gain, "head_weight": head_weight, "draft_probs": draft_probs, "draft_ids": draft_ids, "reject_at": reject_at}


def reference(hidden, gain, head_weight, draft_probs, draft_ids, reject_at):
    values = hidden.astype(jnp.float32)
    squares = lax.optimization_barrier(jnp.sum(values * values, axis=1))
    normed = (values * lax.rsqrt(squares / D + 1e-05)[:, None] * gain.astype(jnp.float32)).astype(jnp.bfloat16)
    block_width = D // N_DP
    logits = jnp.zeros((TOKENS, VOCAB), jnp.float32)
    for block in range(N_DP):
        partial_b = jnp.dot(normed[:, block * block_width:(block + 1) * block_width], head_weight[block * block_width:(block + 1) * block_width], preferred_element_type=jnp.float32)
        logits = logits + partial_b
    top = lax.optimization_barrier(jnp.max(logits, axis=1))
    logz = top + jnp.log(lax.optimization_barrier(jnp.sum(jnp.exp(logits - top[:, None]), axis=1)))
    picked = jnp.take_along_axis(logits, draft_ids.astype(jnp.int32)[:, None], axis=1)[:, 0]
    token_logprob = picked - logz
    where_at = reject_at.astype(jnp.int32)
    grid = logits.reshape(ROWS, POS, VOCAB)
    chosen = jnp.take_along_axis(grid, where_at[:, None, None], axis=1)[:, 0]
    chosen_logz = jnp.take_along_axis(logz.reshape(ROWS, POS), where_at[:, None], axis=1)[:, 0]
    drafts = jnp.take_along_axis(draft_probs.reshape(ROWS, POS, VOCAB), where_at[:, None, None], axis=1)[:, 0]
    target = jnp.exp(chosen - chosen_logz[:, None])
    kept = jnp.maximum(target - drafts, 0.0)
    mass = lax.optimization_barrier(jnp.sum(kept, axis=1))
    residual = VOCAB * kept / mass[:, None]
    return (token_logprob, residual)
```

```python
import functools

import jax
import jax.numpy as jnp
from jax import lax
from jax.experimental import pallas as pl
from jax.experimental.pallas import tpu as pltpu
from jax.sharding import PartitionSpec as P

EPS = 1e-05
CHUNKS = 2
PARTS = 2
TILE = 512
VMEM_LIMIT = 56 * 1024 * 1024
F32 = jnp.float32


def tree_sum(value, axis, count):
    bit = 1
    while bit < count:
        value = value + lax.ppermute(value, axis, [(i, i ^ bit) for i in range(count)])
        bit *= 2
    return value


def merge(first, second):
    top = jnp.maximum(first[0], second[0])
    total = first[1] * jnp.exp(first[0] - top) + second[1] * jnp.exp(second[0] - top)
    return jnp.stack([top, total, first[2] + second[2]])


def tree_merge(stats, axis, count):
    me = lax.axis_index(axis)
    bit = 1
    while bit < count:
        other = lax.ppermute(stats, axis, [(i, i ^ bit) for i in range(count)])
        upper = (me & bit) != 0
        stats = merge(jnp.where(upper, other, stats), jnp.where(upper, stats, other))
        bit *= 2
    return stats


def gather_pieces(piece, nz, nx):
    z = lax.axis_index("tensor") // nx

    def across(found, rows):
        out = [found]
        for k in range(1, nx):
            pairs = [(r * nx + x, r * nx + (x + k) % nx) for r in rows for x in range(nx)]
            out.append(lax.ppermute(found, "tensor", pairs))
        return out

    pieces = [(p, 0, k, z >= 0) for k, p in enumerate(across(piece, range(nz)))]
    up = down = piece
    for far in range(1, nz):
        up = lax.ppermute(
            up, "tensor", [(r * nx + x, (r + 1) * nx + x) for r in range(far - 1, nz - 1) for x in range(nx)]
        )
        down = lax.ppermute(
            down, "tensor", [(r * nx + x, (r - 1) * nx + x) for r in range(1, nz - far + 1) for x in range(nx)]
        )
        pieces += [(p, -far, k, z >= far) for k, p in enumerate(across(up, range(far, nz)))]
        pieces += [(p, far, k, z + far < nz) for k, p in enumerate(across(down, range(0, nz - far)))]
    return pieces


def prepare_kernel(count, holds, place, order, scale, gain, *refs):
    pieces, out = refs[:count], refs[count]
    rows = order.shape[0]
    width = pieces[0].shape[1]
    pick = (lax.broadcasted_iota(jnp.int32, (rows, rows), 1) == order[...]).astype(jnp.bfloat16)
    for n in range(count):

        @pl.when(holds[n] == 1)
        def _(n=n):
            at = place[n]
            normed = (pieces[n][...].astype(F32) * scale[...] * gain[pl.ds(at, 1), :]).astype(jnp.bfloat16)
            moved = jnp.dot(pick, normed, preferred_element_type=F32).astype(jnp.bfloat16)
            out[:, pl.ds(pl.multiple_of(at * width, width), width)] = moved


def prepare(pieces, holds, place, order, scale, gain, depth):
    rows = order.shape[0]
    smem = pl.BlockSpec(memory_space=pltpu.SMEM)
    vmem = pl.BlockSpec(memory_space=pltpu.VMEM)
    return pl.pallas_call(
        functools.partial(prepare_kernel, len(pieces)),
        out_shape=jax.ShapeDtypeStruct((rows, depth), jnp.bfloat16),
        in_specs=[smem, smem] + [vmem] * (3 + len(pieces)),
        out_specs=vmem,
        compiler_params=pltpu.CompilerParams(vmem_limit_bytes=VMEM_LIMIT),
        cost_estimate=pl.CostEstimate(
            flops=2 * rows * rows * depth, bytes_accessed=6 * rows * depth, transcendentals=0
        ),
        name="prepare",
    )(holds, place, order, scale, gain, *pieces)


def head_kernel(x, w, send, keep):
    half = send.shape[0]
    out = jnp.dot(x[...], w[...], preferred_element_type=F32)
    send[...] = out[:half]
    keep[...] = out[half:]


def head(normed, weight, first, width):
    rows, depth = normed.shape
    tile = min(TILE, width)
    half = jax.ShapeDtypeStruct((rows // 2, width), F32)
    spec = pl.BlockSpec((rows // 2, tile), lambda j: (0, j))
    return pl.pallas_call(
        head_kernel,
        out_shape=(half, half),
        grid=(width // tile,),
        in_specs=[
            pl.BlockSpec((rows, depth), lambda j: (0, 0)),
            pl.BlockSpec((depth, tile), lambda j: (0, first // tile + j)),
        ],
        out_specs=(spec, spec),
        compiler_params=pltpu.CompilerParams(vmem_limit_bytes=VMEM_LIMIT),
        cost_estimate=pl.CostEstimate(
            flops=2 * rows * depth * width,
            bytes_accessed=2 * depth * width + 2 * rows * depth + 4 * rows * width,
            transcendentals=0,
        ),
        name="head",
    )(normed, weight)


def encode_kernel(keep, came, coded, info):
    total = keep[...] + came[...]
    high = jnp.max(total, axis=1, keepdims=True)
    low = jnp.min(total, axis=1, keepdims=True)
    middle = 0.5 * high + 0.5 * low
    step = jnp.maximum((0.5 * high - 0.5 * low) * (1.0 / 32700.0), 1e-30)
    scaled = (total - middle) * (1.0 / step)
    coded[...] = jnp.floor(scaled + 0.5).astype(jnp.int32).astype(jnp.int16)
    lanes = lax.broadcasted_iota(jnp.int32, info.shape, 1)
    info[...] = jnp.where(lanes < info.shape[1] // 2, middle, step)


def encode(keep, came, first, count, block):
    width = keep.shape[1]
    source = pl.BlockSpec((block, width), lambda i: (first // block + i, 0))
    return pl.pallas_call(
        encode_kernel,
        out_shape=(
            jax.ShapeDtypeStruct((count, width), jnp.int16),
            jax.ShapeDtypeStruct((count, 128), F32),
        ),
        grid=(count // block,),
        in_specs=[source, source],
        out_specs=(
            pl.BlockSpec((block, width), lambda i: (i, 0)),
            pl.BlockSpec((block, 128), lambda i: (i, 0)),
        ),
        cost_estimate=pl.CostEstimate(
            flops=8 * count * width, bytes_accessed=10 * count * width, transcendentals=0
        ),
        name="encode",
    )(keep, came)


def finish_kernel(others, ids, keep, came, *refs):
    total = keep[...] + came[...]
    for n in range(others):
        info = refs[2 * n + 1][...]
        middle, step = info[:, :1], info[:, 127:]
        total = total + (refs[2 * n][...].astype(jnp.int32).astype(F32) * step + middle)
    stats = refs[2 * others]
    top = jnp.max(total, axis=1, keepdims=True)
    sums = jnp.sum(jnp.exp(total - top), axis=1, keepdims=True)
    columns = lax.broadcasted_iota(jnp.int32, total.shape, 1)
    picked = jnp.sum(jnp.where(columns == ids[...], total, 0.0), axis=1, keepdims=True)
    lanes = lax.broadcasted_iota(jnp.int32, stats.shape, 1)
    stats[...] = jnp.where(lanes == 0, top, jnp.where(lanes == 1, sums, picked))


def finish(ids, keep, came, arrived, first, block):
    count, width = ids.shape[0], keep.shape[1]
    own = pl.BlockSpec((block, width), lambda i: (first // block + i, 0))
    specs, args = [], []
    for coded, info in arrived:
        specs += [
            pl.BlockSpec((block, width), lambda i: (i, 0)),
            pl.BlockSpec((block, 128), lambda i: (i, 0)),
        ]
        args += [coded, info]
    return pl.pallas_call(
        functools.partial(finish_kernel, len(arrived)),
        out_shape=jax.ShapeDtypeStruct((count, 128), F32),
        grid=(count // block,),
        in_specs=[pl.BlockSpec((block, 1), lambda i: (i, 0)), own, own] + specs,
        out_specs=pl.BlockSpec((block, 128), lambda i: (i, 0)),
        cost_estimate=pl.CostEstimate(
            flops=12 * count * width, bytes_accessed=10 * count * width, transcendentals=count * width
        ),
        name="finish",
    )(ids, keep, came, *args)


def select_kernel(positions, at, drafts, out):
    for r in range(out.shape[1]):
        out[0, pl.ds(r, 1), :] = drafts[pl.ds(r * positions + at[r], 1), :]


def select_drafts(drafts, at, positions, count):
    rows, vocab = drafts.shape
    width = vocab // count
    return pl.pallas_call(
        functools.partial(select_kernel, positions),
        out_shape=jax.ShapeDtypeStruct((count, rows // positions, width), F32),
        grid=(count,),
        in_specs=[
            pl.BlockSpec(memory_space=pltpu.SMEM),
            pl.BlockSpec((rows, width), lambda j: (0, j)),
        ],
        out_specs=pl.BlockSpec((1, rows // positions, width), lambda j: (j, 0, 0)),
        cost_estimate=pl.CostEstimate(flops=0, bytes_accessed=5 * rows * vocab, transcendentals=0),
        name="select_drafts",
    )(at, drafts)


def shards(n_dp, n_tensor, hidden, gain, head_weight, draft_probs, draft_ids, reject_at):
    tokens, local = hidden.shape
    features = local * n_dp * n_tensor
    depth, width = head_weight.shape
    vocab = width * n_tensor
    requests = reject_at.shape[0]
    owned = draft_ids.shape[0]
    positions = owned // requests
    n_y = n_dp // 2
    nx = 1
    while nx * nx * 4 <= n_tensor:
        nx *= 2
    nz = n_tensor // nx
    d, t = lax.axis_index("dp"), lax.axis_index("tensor")
    y, c = d // 2, d % 2
    z, x = t // nx, t % nx

    values = hidden.astype(F32)
    squares = jnp.sum(values * values, axis=1)
    places = lax.dynamic_update_slice(jnp.zeros((n_dp * requests,), F32), reject_at.astype(F32), (d * requests,))
    small = jnp.concatenate([squares, places])
    short = -small.shape[0] % 1024
    small = tree_sum(jnp.pad(small, (0, short)).reshape(-1, 128), "dp", n_dp)
    flat = small.reshape(-1)
    every_at = flat[tokens : tokens + n_dp * requests].astype(jnp.int32).reshape(n_dp, requests)
    gains = lax.dynamic_update_slice(jnp.zeros((depth,), F32), gain[0].astype(F32), (t * local,))
    small = jnp.concatenate([flat[:tokens], gains])
    small = jnp.pad(small, (0, -small.shape[0] % 1024)).reshape(-1, 128)
    flat = tree_sum(small, "tensor", n_tensor).reshape(-1)
    scale = lax.rsqrt(flat[:tokens] / features + EPS)
    gains = flat[tokens : tokens + depth]

    rq = requests // CHUNKS
    rpo = rq * positions
    rows = n_dp * rpo
    by_owner = hidden.reshape(n_dp, owned, local)
    relayed = local % 128 == 0
    gathered = []
    for chunk in range(CHUNKS):
        piece = by_owner[:, chunk * rpo : (chunk + 1) * rpo].reshape(rows, local)
        if relayed:
            gathered.append(gather_pieces(piece, nz, nx))
        else:
            whole = lax.all_gather(piece, "tensor", axis=1, tiled=True)
            gathered.append([(whole, 0, 0, z >= 0)])
    piece_width = local if relayed else depth
    gains = gains.reshape(-1, piece_width)

    pad16 = rq
    rest = rpo - rq
    r_at = jnp.arange(rest) // (positions - 1)
    k_at = jnp.arange(rest) % (positions - 1)

    def rows_of(at):
        chosen = jnp.arange(rq) * positions + at
        there = at[r_at]
        return jnp.concatenate([chosen, r_at * positions + k_at + (k_at >= there)]).astype(jnp.int32)

    hops = [k % n_y for k in range(1, n_y + 1)]
    block = 16 if rest % 16 == 0 and rq % 16 == 0 else rq
    own_at = (n_y - 1) * rpo
    part = width // PARTS
    chosen_logits, chosen_stats, other_stats, own_rows = [], [], [], []
    far_chosen = {}
    core_pairs = [(i, i ^ 1) for i in range(n_dp)]

    def y_pairs(k):
        return [(i, ((i // 2 + k) % n_y) * 2 + i % 2) for i in range(n_dp)]

    for chunk in range(CHUNKS):
        order = []
        for core in (1 - c, c):
            for k in hops:
                owner = ((y + k) % n_y) * 2 + core
                at = lax.dynamic_slice(every_at, (owner, chunk * rq), (1, rq))[0]
                order.append(owner * rpo + rows_of(at))
        order = jnp.concatenate(order)[:, None].astype(jnp.int32)
        pieces = gathered[chunk]
        if relayed:
            place = jnp.stack([(z + dz) * nx + (x - k) % nx for _, dz, k, _ in pieces]).astype(jnp.int32)
        else:
            place = jnp.zeros((1,), jnp.int32)
        holds = jnp.stack([h for *_, h in pieces]).astype(jnp.int32)
        place = jnp.where(holds == 1, place, 0)
        chunk_scale = scale.reshape(n_dp, owned)[:, chunk * rpo : (chunk + 1) * rpo].reshape(rows, 1)
        normed = prepare([p for p, *_ in pieces], holds, place, order, chunk_scale, gains, depth)
        mine = rows_of(reject_at[chunk * rq : (chunk + 1) * rq])
        own_rows.append(mine + chunk * rpo)
        ids = draft_ids[chunk * rpo : (chunk + 1) * rpo][mine][:, None] - t * width
        for p in range(PARTS):
            send, keep = head(normed, head_weight, p * part, part)
            came = lax.ppermute(send, "dp", core_pairs)
            arrived, chosen_far = [], None
            for n, k in enumerate(hops[:-1]):
                at = n * rpo
                leaving = keep[at : at + rq] + came[at : at + rq]
                got = lax.ppermute(leaving, "dp", y_pairs(k))
                chosen_far = got if chosen_far is None else chosen_far + got
                coded, info = encode(keep, came, at + rq, rest, block)
                arrived.append(
                    (lax.ppermute(coded, "dp", y_pairs(k)), lax.ppermute(info, "dp", y_pairs(k)))
                )
            part_ids = ids - p * part
            logits = keep[own_at : own_at + rq] + came[own_at : own_at + rq]
            if chosen_far is not None:
                logits = logits + chosen_far
            chosen_logits.append(logits)
            top = jnp.max(logits, axis=1)
            sums = jnp.sum(jnp.exp(logits - top[:, None]), axis=1)
            columns = lax.broadcasted_iota(jnp.int32, (1, part), 1)
            picked = jnp.sum(jnp.where(columns == part_ids[:rq], logits, 0.0), axis=1)
            chosen_stats.append(jnp.stack([top, sums, picked]))
            stats = finish(part_ids[rq:], keep, came, arrived, own_at + rq, block)
            other_stats.append(stats[:, :3].T)

    def joined(stats):
        chunks = []
        for chunk in range(CHUNKS):
            merged = stats[chunk * PARTS]
            for p in range(1, PARTS):
                merged = merge(merged, stats[chunk * PARTS + p])
            chunks.append(merged)
        return jnp.concatenate(chunks, axis=1)

    of_chosen = tree_merge(joined(chosen_stats), "tensor", n_tensor)
    chosen_logz = of_chosen[0] + jnp.log(of_chosen[1])

    mine = requests // n_tensor
    at = lax.dynamic_slice(reject_at, (t * mine,), (mine,))
    drafts = select_drafts(draft_probs, at, positions, n_tensor)
    drafts, _ = lax.optimization_barrier((drafts, gathered[-1][-1][0]))
    drafts = lax.all_to_all(drafts, "tensor", split_axis=0, concat_axis=0, tiled=True).reshape(requests, width)

    logits = jnp.concatenate(
        [
            jnp.concatenate(chosen_logits[chunk * PARTS : (chunk + 1) * PARTS], axis=1)
            for chunk in range(CHUNKS)
        ]
    )
    kept = jnp.maximum(jnp.exp(logits - chosen_logz[:, None]) - drafts, 0.0)
    mass = tree_sum(jnp.sum(kept, axis=1), "tensor", n_tensor)
    residual = vocab * kept / mass[:, None]

    of_other = tree_merge(joined(other_stats), "tensor", n_tensor)
    chosen_logprob = of_chosen[2] - chosen_logz
    other_logprob = of_other[2] - (of_other[0] + jnp.log(of_other[1]))
    found = jnp.concatenate(
        [
            jnp.concatenate(
                [chosen_logprob[chunk * rq : (chunk + 1) * rq], other_logprob[chunk * rest : (chunk + 1) * rest]]
            )
            for chunk in range(CHUNKS)
        ]
    )
    where = jnp.concatenate(own_rows)
    token_logprob = jnp.sum(
        jnp.where(where[None, :] == jnp.arange(owned)[:, None], found[None, :], 0.0), axis=1
    )
    return (token_logprob, residual)


def solution(mesh):
    return jax.shard_map(
        functools.partial(shards, mesh.shape["dp"], mesh.shape["tensor"]),
        mesh=mesh,
        in_specs=(
            P(None, ("dp", "tensor")),
            P(None, ("dp", "tensor")),
            P("dp", "tensor"),
            P(("dp", "tensor"), None),
            P("dp"),
            P("dp"),
        ),
        out_specs=(P("dp"), P("dp", "tensor")),
        check_vma=False,
    )
```

```python
import functools

import jax
import jax.numpy as jnp
from jax import lax
from jax.experimental import pallas as pl
from jax.experimental.pallas import tpu as pltpu
from jax.sharding import PartitionSpec as P

EPS = 1e-05
FIRST_PARTS = (2, 2)
REST_PARTS = (2, 1, 1)
ROWS = 32
TILES = 1024, 512
VMEM_LIMIT = 56 * 1024 * 1024
F32 = jnp.float32
COST = pl.CostEstimate(flops=1024, bytes_accessed=1024, transcendentals=0)


def tree_sum(value, axis, count):
    bit = 1
    while bit < count:
        value = value + lax.ppermute(value, axis, [(i, i ^ bit) for i in range(count)])
        bit *= 2
    return value


def merge(first, second):
    top = jnp.maximum(first[0], second[0])
    total = first[1] * jnp.exp(first[0] - top) + second[1] * jnp.exp(second[0] - top)
    return jnp.stack([top, total, first[2] + second[2]])


def tree_merge(stats, axis, count):
    me = lax.axis_index(axis)
    bit = 1
    while bit < count:
        other = lax.ppermute(stats, axis, [(i, i ^ bit) for i in range(count)])
        upper = (me & bit) != 0
        stats = merge(jnp.where(upper, other, stats), jnp.where(upper, stats, other))
        bit *= 2
    return stats


def held_after(value, *earlier):
    if not earlier:
        return value
    return lax.optimization_barrier((value,) + earlier)[0]


def gather_pieces(piece, nz, nx, during=()):
    count = nz * nx

    def step(value, bits):
        return lax.ppermute(value, "tensor", [(i, i ^ bits) for i in range(count)])

    along = {0: piece}
    bit = nz // 2
    while bit:
        for offset in sorted(along):
            along[offset | bit] = step(held_after(along[offset], *during) if offset else piece, bit * nx)
        bit //= 2
    pieces = {(offset, 0): value for offset, value in along.items()}
    for k in range(1, nx):
        first = step(along[0], k)
        pieces[0, k] = first
        for offset in range(1, nz):
            pieces[offset, k] = step(along[offset], k)
    return pieces


def prepare_kernel(count, place, order, scale, gain, *refs):
    pieces, out = refs[:count], refs[count]
    rows, width = pieces[0].shape
    pick = (lax.broadcasted_iota(jnp.int32, (order.shape[0], rows), 1) == order[...]).astype(jnp.bfloat16)
    for n in range(count):
        at = place[n]
        normed = (pieces[n][...].astype(F32) * scale[...] * gain[pl.ds(at, 1), :]).astype(jnp.bfloat16)
        moved = jnp.dot(pick, normed, preferred_element_type=F32).astype(jnp.bfloat16)
        out[:, pl.ds(pl.multiple_of(at * width, width), width)] = moved


def prepare(pieces, place, order, scale, gain, depth):
    rows = order.shape[0]
    smem = pl.BlockSpec(memory_space=pltpu.SMEM)
    vmem = pl.BlockSpec(memory_space=pltpu.VMEM)
    return pl.pallas_call(
        functools.partial(prepare_kernel, len(pieces)),
        out_shape=jax.ShapeDtypeStruct((rows, depth), jnp.bfloat16),
        in_specs=[smem] + [vmem] * (3 + len(pieces)),
        out_specs=vmem,
        compiler_params=pltpu.CompilerParams(vmem_limit_bytes=VMEM_LIMIT),
        cost_estimate=COST,
        name="prepare",
    )(place, order, scale, gain, *pieces)


def head_kernel(x, w, send, keep):
    half = send.shape[0]
    out = jnp.dot(x[...], w[...], preferred_element_type=F32)
    send[...] = out[:half]
    keep[...] = out[half:]


def head(normed, weight, first, width, tile):
    rows, depth = normed.shape
    tile = min(tile, width)
    half = jax.ShapeDtypeStruct((rows // 2, width), F32)
    spec = pl.BlockSpec((rows // 2, tile), lambda j: (0, j))
    return pl.pallas_call(
        head_kernel,
        out_shape=(half, half),
        grid=(width // tile,),
        in_specs=[
            pl.BlockSpec((rows, depth), lambda j: (0, 0)),
            pl.BlockSpec((depth, tile), lambda j: (0, first // tile + j)),
        ],
        out_specs=(spec, spec),
        compiler_params=pltpu.CompilerParams(vmem_limit_bytes=VMEM_LIMIT),
        cost_estimate=pl.CostEstimate(
            flops=16 * rows * depth * width, bytes_accessed=2 * depth * width, transcendentals=0
        ),
        name="head",
    )(normed, weight)


def exponent(value):
    return jnp.floor(jnp.log2(jnp.maximum(value * 1.001, 1e-20))) + 1.0


def encode_kernel(keep, came, coded):
    rows, width = keep.shape
    lanes = lax.broadcasted_iota(jnp.int32, (rows, 128), 1)
    total = keep[...] + came[...]
    high = jnp.max(total, axis=1, keepdims=True)
    low = jnp.min(total, axis=1, keepdims=True)
    middle = 0.5 * high + 0.5 * low
    shift = exponent(jnp.abs(middle))
    unit = jnp.floor(middle * jnp.exp2(15.0 - shift) + 0.5)
    middle = unit * jnp.exp2(shift - 15.0)
    size = exponent(jnp.maximum(high - middle, middle - low))
    scaled = (total - middle) * jnp.exp2(15.0 - size)
    coded[:, :width] = jnp.floor(scaled + 0.5).astype(jnp.int32).astype(jnp.int16)
    info = jnp.where(lanes == 0, unit, jnp.where(lanes == 1, shift, size))
    coded[:, width:] = info.astype(jnp.int32).astype(jnp.int16)


def encode(keep, came, group, count):
    width = keep.shape[1]
    steps = count // ROWS
    source = pl.BlockSpec((ROWS, width), lambda i: (group * steps + i, 0))
    return pl.pallas_call(
        encode_kernel,
        out_shape=jax.ShapeDtypeStruct((count, width + 128), jnp.int16),
        grid=(steps,),
        in_specs=[source, source],
        out_specs=pl.BlockSpec((ROWS, width + 128), lambda i: (i, 0)),
        compiler_params=pltpu.CompilerParams(vmem_limit_bytes=VMEM_LIMIT),
        cost_estimate=COST,
        name="encode",
    )(keep, came)


def row_stats(total, ids):
    top = jnp.max(total, axis=1, keepdims=True)
    sums = jnp.sum(jnp.exp(total - top), axis=1, keepdims=True)
    columns = lax.broadcasted_iota(jnp.int32, total.shape, 1)
    picked = jnp.sum(jnp.where(columns == ids, total, 0.0), axis=1, keepdims=True)
    lanes = lax.broadcasted_iota(jnp.int32, (total.shape[0], 128), 1)
    return jnp.where(lanes == 0, top, jnp.where(lanes == 1, sums, picked))


def finish_chosen_kernel(far, ids, keep, came, *refs):
    total = keep[...] + came[...]
    for wide in refs[:far]:
        total = total + wide[:, : total.shape[1]]
    logits, stats = refs[far:]
    logits[...] = total
    stats[...] = row_stats(total, ids[...])


def finish_others_kernel(far, ids, keep, came, *refs):
    width = keep.shape[1]
    total = keep[...] + came[...]
    for coded in refs[:far]:
        info = coded[:, width:].astype(jnp.int32).astype(F32)
        middle = info[:, :1] * jnp.exp2(info[:, 1:2] - 15.0)
        step = jnp.exp2(info[:, 2:3] - 15.0)
        total = total + (coded[:, :width].astype(jnp.int32).astype(F32) * step + middle)
    refs[far][...] = row_stats(total, ids[...])


def finish_chosen(ids, keep, came, wides, first):
    count, width = ids.shape[0], keep.shape[1]
    own = pl.BlockSpec((count, width), lambda i: (first // count, 0))
    return pl.pallas_call(
        functools.partial(finish_chosen_kernel, len(wides)),
        out_shape=(jax.ShapeDtypeStruct((count, width), F32), jax.ShapeDtypeStruct((count, 128), F32)),
        grid=(1,),
        in_specs=[pl.BlockSpec((count, 1), lambda i: (0, 0)), own, own]
        + [pl.BlockSpec((count, width), lambda i: (0, 0)) for _ in wides],
        out_specs=(
            pl.BlockSpec((count, width), lambda i: (0, 0)),
            pl.BlockSpec((count, 128), lambda i: (0, 0)),
        ),
        cost_estimate=COST,
        name="finish_chosen",
    )(ids, keep, came, *wides)


def finish_others(ids, keep, came, codeds, group):
    count, width = ids.shape[0], keep.shape[1]
    steps = count // ROWS
    own = pl.BlockSpec((ROWS, width), lambda i: (group * steps + i, 0))
    return pl.pallas_call(
        functools.partial(finish_others_kernel, len(codeds)),
        out_shape=jax.ShapeDtypeStruct((count, 128), F32),
        grid=(steps,),
        in_specs=[pl.BlockSpec((ROWS, 1), lambda i: (i, 0)), own, own]
        + [pl.BlockSpec((ROWS, width + 128), lambda i: (i, 0)) for _ in codeds],
        out_specs=pl.BlockSpec((ROWS, 128), lambda i: (i, 0)),
        compiler_params=pltpu.CompilerParams(vmem_limit_bytes=VMEM_LIMIT),
        cost_estimate=COST,
        name="finish_others",
    )(ids, keep, came, *codeds)


def select_kernel(positions, at, drafts, out):
    for r in range(out.shape[1]):
        out[0, pl.ds(r, 1), :] = drafts[pl.ds(r * positions + at[r], 1), :]


def select_drafts(drafts, at, positions, count):
    rows, vocab = drafts.shape
    width = vocab // count
    return pl.pallas_call(
        functools.partial(select_kernel, positions),
        out_shape=jax.ShapeDtypeStruct((count, rows // positions, width), F32),
        grid=(count,),
        in_specs=[
            pl.BlockSpec(memory_space=pltpu.SMEM),
            pl.BlockSpec((rows, width), lambda j: (0, j)),
        ],
        out_specs=pl.BlockSpec((1, rows // positions, width), lambda j: (j, 0, 0)),
        cost_estimate=COST,
        name="select_drafts",
    )(at, drafts)


def shards(n_dp, n_tensor, hidden, gain, head_weight, draft_probs, draft_ids, reject_at):
    tokens, local = hidden.shape
    features = local * n_dp * n_tensor
    depth, width = head_weight.shape
    vocab = width * n_tensor
    requests = reject_at.shape[0]
    owned = draft_ids.shape[0]
    positions = owned // requests
    n_y = n_dp // 2
    nx = 1
    while nx * nx * 4 <= n_tensor:
        nx *= 2
    nz = n_tensor // nx
    d, t = lax.axis_index("dp"), lax.axis_index("tensor")
    y, c = d // 2, d % 2
    z, x = t // nx, t % nx

    relayed = local % 128 == 0
    if relayed:
        whole = gather_pieces(hidden, nz, nx)
    else:
        whole = {(0, 0): lax.all_gather(hidden, "tensor", axis=1, tiled=True)}
    offsets = list(whole)

    values = hidden.astype(F32)
    squares = jnp.sum(values * values, axis=1)
    places = lax.dynamic_update_slice(jnp.zeros((n_dp * requests,), F32), reject_at.astype(F32), (d * requests,))
    small = jnp.concatenate([squares, places])
    short = -small.shape[0] % 1024
    small = tree_sum(jnp.pad(small, (0, short)).reshape(-1, 128), "dp", n_dp)
    flat = small.reshape(-1)
    every_at = flat[tokens : tokens + n_dp * requests].astype(jnp.int32).reshape(n_dp, requests)
    gains = lax.dynamic_update_slice(jnp.zeros((depth,), F32), gain[0].astype(F32), (t * local,))
    small = jnp.concatenate([flat[:tokens], gains])
    small = jnp.pad(small, (0, -small.shape[0] % 1024)).reshape(-1, 128)
    flat = tree_sum(small, "tensor", n_tensor).reshape(-1)
    scale = lax.rsqrt(flat[:tokens] / features + EPS)
    gains = flat[tokens : tokens + depth]

    turn = []

    def next_turn(value):
        return held_after(value, turn[-1]) if turn else value

    mine = requests // n_tensor
    at = lax.dynamic_slice(reject_at, (t * mine,), (mine,))
    drafts = select_drafts(draft_probs, at, positions, n_tensor)

    rest = owned - requests
    starts = jnp.arange(requests, dtype=jnp.int32) * positions
    steps = jnp.arange(positions - 1, dtype=jnp.int32)

    def chosen_of(at):
        return starts + at

    def others_of(at):
        return (starts[:, None] + steps + (steps >= at[..., None])).reshape(at.shape[:-1] + (rest,))

    owners = jnp.arange(n_dp, dtype=jnp.int32)[:, None]
    chosen_tokens = (owners * owned + chosen_of(every_at)).reshape(-1)
    is_chosen = chosen_tokens[:, None] == jnp.arange(tokens)
    piece = jnp.dot(is_chosen.astype(jnp.bfloat16), hidden, preferred_element_type=F32).astype(jnp.bfloat16)
    chosen_scale = jnp.sum(jnp.where(is_chosen, scale, 0.0), axis=1)
    if relayed:
        gathered = gather_pieces(piece, nz, nx, (drafts,))
    else:
        gathered = {(0, 0): lax.all_gather(piece, "tensor", axis=1, tiled=True)}

    hops = [k % n_y for k in range(1, n_y + 1)]
    groups = jnp.stack([((y + k) % n_y) * 2 + core for core in (1 - c, c) for k in hops])
    is_group = (groups[:, None] == jnp.arange(n_dp))[:, :, None]

    def grouped(of_owner):
        return jnp.sum(jnp.where(is_group, of_owner, 0), axis=1).reshape(-1, 1).astype(jnp.int32)

    core_pairs = [(i, i ^ 1) for i in range(n_dp)]

    def y_pairs(k):
        return [(i, ((i // 2 + k) % n_y) * 2 + i % 2) for i in range(n_dp)]

    where = jnp.concatenate([chosen_of(reject_at), others_of(reject_at)])
    ids = jnp.sum(jnp.where(where[:, None] == jnp.arange(owned), draft_ids, 0), axis=1) - t * width
    ids = ids[:, None]

    def span(parts, p):
        quarter = width // sum(parts)
        return sum(parts[:p]) * quarter, parts[p] * quarter

    def do_head(normed, p, parts, tile):
        send, keep = head(next_turn(normed), head_weight, *span(parts, p), tile)
        turn.append(keep)
        return keep, lax.ppermute(send, "dp", core_pairs)

    place = jnp.stack([((z ^ dz) * nx + (x ^ k)) if relayed else 0 * z for dz, k in offsets]).astype(jnp.int32)
    order = grouped(owners * requests + jnp.arange(requests, dtype=jnp.int32))
    by_piece = gains.reshape(-1, local if relayed else depth)

    def met(*at):
        return tuple(whole[o] for o in at) if relayed and nz > 2 and nx == 2 else ()

    normed = prepare(
        [gathered[o] for o in offsets],
        place,
        held_after(next_turn(order), *met((1, 0), (2, 0), (0, 1), (1, 1))),
        chosen_scale[:, None],
        by_piece,
        depth,
    )
    turn.append(normed)
    first_heads = [do_head(normed, 0, FIRST_PARTS, TILES[0])]
    normed = held_after(normed, *met((3, 0), (2, 1)))
    for p in range(1, len(FIRST_PARTS)):
        first_heads.append(do_head(normed, p, FIRST_PARTS, TILES[0]))
    chosen_far = []

    def send_chosen(p):
        keep, came = first_heads[p]
        keep = next_turn(keep)
        leaving = [
            keep[n * requests : (n + 1) * requests] + came[n * requests : (n + 1) * requests]
            for n in range(n_y - 1)
        ]
        chosen_far.append([lax.ppermute(v, "dp", y_pairs(k)) for k, v in zip(hops, leaving)])
        turn.extend(leaving[-1:])

    chosen_logits, chosen_stats = [], []

    def do_chosen(p):
        keep, came = first_heads[p]
        part_ids = next_turn(ids[:requests] - span(FIRST_PARTS, p)[0])
        logits, stats = finish_chosen(part_ids, keep, came, chosen_far[p], (n_y - 1) * requests)
        chosen_logits.append(logits)
        chosen_stats.append(stats)
        turn.append(stats)

    for p in range(len(FIRST_PARTS) - 1):
        send_chosen(p)

    order = grouped(owners * owned + others_of(every_at))
    normed = prepare([whole[o] for o in offsets], place, next_turn(order), scale[:, None], by_piece, depth)
    turn.append(normed)
    send_chosen(len(FIRST_PARTS) - 1)
    drafts = held_after(drafts, normed)
    drafts = lax.all_to_all(drafts, "tensor", split_axis=0, concat_axis=0, tiled=True)
    rest_heads, coded_far, other_stats = [], [], []

    def send_others(p):
        keep, came = rest_heads[p]
        far = []
        for n, k in enumerate(hops[:-1]):
            coded = encode(next_turn(keep), came, n, rest)
            turn.append(coded)
            far.append(lax.ppermute(coded, "dp", y_pairs(k)))
        coded_far.append(far)

    def do_others(p):
        keep, came = rest_heads[p]
        part_ids = next_turn(ids[requests:] - span(REST_PARTS, p)[0])
        other_stats.append(finish_others(part_ids, keep, came, coded_far[p], n_y - 1))
        turn.append(other_stats[-1])

    for p in range(len(REST_PARTS)):
        rest_heads.append(do_head(normed, p, REST_PARTS, TILES[1]))
        if p == 0:
            turn.append(drafts)
            for q in range(len(FIRST_PARTS)):
                do_chosen(q)
        else:
            send_others(p - 1)
    for p in range(len(REST_PARTS) - 2):
        do_others(p)
    send_others(len(REST_PARTS) - 1)
    sent_last = turn[-1]
    for p in range(max(len(REST_PARTS) - 2, 0), len(REST_PARTS)):
        do_others(p)

    def joined(stats):
        merged = stats[0][:, :3].T
        for other in stats[1:]:
            merged = merge(merged, other[:, :3].T)
        return merged

    of_chosen = tree_merge(joined(chosen_stats), "tensor", n_tensor)
    chosen_logz = of_chosen[0] + jnp.log(of_chosen[1])
    logits = held_after(jnp.concatenate(chosen_logits, axis=1), sent_last)
    kept = jnp.maximum(jnp.exp(logits - chosen_logz[:, None]) - drafts.reshape(requests, width), 0.0)
    mass = jnp.sum(kept, axis=1)
    zero = jnp.zeros_like(mass)
    of_other = jnp.concatenate([joined(other_stats), jnp.stack([zero, mass, zero])], axis=1)
    of_other = tree_merge(of_other, "tensor", n_tensor)
    mass = of_other[1, rest:]
    of_other = of_other[:, :rest]
    residual = vocab * kept / mass[:, None]
    found = jnp.concatenate(
        [of_chosen[2] - chosen_logz, of_other[2] - (of_other[0] + jnp.log(of_other[1]))]
    )
    token_logprob = jnp.sum(
        jnp.where(where[None, :] == jnp.arange(owned)[:, None], found[None, :], 0.0), axis=1
    )
    return (token_logprob, residual)


def solution(mesh):
    return jax.shard_map(
        functools.partial(shards, mesh.shape["dp"], mesh.shape["tensor"]),
        mesh=mesh,
        in_specs=(
            P(None, ("dp", "tensor")),
            P(None, ("dp", "tensor")),
            P("dp", "tensor"),
            P(("dp", "tensor"), None),
            P("dp"),
            P("dp"),
        ),
        out_specs=(P("dp"), P("dp", "tensor")),
        check_vma=False,
    )
```

```python
import functools

import jax
import jax.numpy as jnp
from jax import lax
from jax.experimental import pallas as pl
from jax.experimental.pallas import tpu as pltpu
from jax.sharding import PartitionSpec as P

EPS = 1e-05
FIRST_PARTS = (2, 2)
REST_PARTS = (2, 1, 1)
ROWS = 32
TILES = 1024, 512
VMEM_LIMIT = 56 * 1024 * 1024
F32 = jnp.float32
COST = pl.CostEstimate(flops=1024, bytes_accessed=1024, transcendentals=0)


def tree_sum(value, axis, count):
    bit = 1
    while bit < count:
        value = value + lax.ppermute(value, axis, [(i, i ^ bit) for i in range(count)])
        bit *= 2
    return value


def merge(first, second):
    top = jnp.maximum(first[0], second[0])
    total = first[1] * jnp.exp(first[0] - top) + second[1] * jnp.exp(second[0] - top)
    return jnp.stack([top, total, first[2] + second[2]])


def tree_merge(stats, axis, count):
    me = lax.axis_index(axis)
    bit = 1
    while bit < count:
        other = lax.ppermute(stats, axis, [(i, i ^ bit) for i in range(count)])
        upper = (me & bit) != 0
        stats = merge(jnp.where(upper, other, stats), jnp.where(upper, stats, other))
        bit *= 2
    return stats


def held_after(value, *earlier):
    if not earlier:
        return value
    return lax.optimization_barrier((value,) + earlier)[0]


def gather_pieces(piece, nz, nx, first, during):
    count = nz * nx

    def step(value, bits):
        return lax.ppermute(value, "tensor", [(i, i ^ bits) for i in range(count)])

    pieces = {(0, 0): piece}
    bit = nz // 2
    while bit:
        pieces[bit, 0] = step(piece, bit * nx)
        bit //= 2
    for k in range(1, nx):
        pieces[0, k] = step(held_after(piece, first), k)
        pieces[1, k] = step(held_after(pieces[1, 0], pieces[0, k]), k)
    done = [0, 1]
    for offset in range(2, nz):
        near = offset & -offset
        if (offset, 0) not in pieces:
            before = [pieces[o, k] for o in done for k in range(1, nx)] + [during]
            pieces[offset, 0] = step(held_after(pieces[offset - near, 0], *before), near * nx)
        for k in range(1, nx):
            ahead = (pieces[offset - 1, k],) if offset > 2 else ()
            pieces[offset, k] = step(held_after(pieces[offset, 0], *ahead), k)
    return pieces


def prepare_kernel(count, place, order, scale, gain, *refs):
    pieces, (chosen, others) = refs[:count], refs[count:]
    first = chosen.shape[0]
    rows, width = pieces[0].shape
    pick = (lax.broadcasted_iota(jnp.int32, (order.shape[0], rows), 1) == order[...]).astype(jnp.bfloat16)
    for n in range(count):
        at = place[n]
        normed = (pieces[n][...].astype(F32) * scale[...] * gain[pl.ds(at, 1), :]).astype(jnp.bfloat16)
        moved = jnp.dot(pick, normed, preferred_element_type=F32).astype(jnp.bfloat16)
        columns = pl.ds(pl.multiple_of(at * width, width), width)
        chosen[:, columns] = moved[:first]
        others[:, columns] = moved[first:]


def prepare(pieces, place, order, scale, gain, depth, first):
    rows = order.shape[0]
    smem = pl.BlockSpec(memory_space=pltpu.SMEM)
    vmem = pl.BlockSpec(memory_space=pltpu.VMEM)
    return pl.pallas_call(
        functools.partial(prepare_kernel, len(pieces)),
        out_shape=(
            jax.ShapeDtypeStruct((first, depth), jnp.bfloat16),
            jax.ShapeDtypeStruct((rows - first, depth), jnp.bfloat16),
        ),
        in_specs=[smem] + [vmem] * (3 + len(pieces)),
        out_specs=(vmem, vmem),
        compiler_params=pltpu.CompilerParams(vmem_limit_bytes=VMEM_LIMIT),
        cost_estimate=COST,
        name="prepare",
    )(place, order, scale, gain, *pieces)


def head_kernel(x, w, send, keep):
    half = send.shape[0]
    out = jnp.dot(x[...], w[...], preferred_element_type=F32)
    send[...] = out[:half]
    keep[...] = out[half:]


def head(normed, weight, first, width, tile):
    rows, depth = normed.shape
    tile = min(tile, width)
    half = jax.ShapeDtypeStruct((rows // 2, width), F32)
    spec = pl.BlockSpec((rows // 2, tile), lambda j: (0, j))
    return pl.pallas_call(
        head_kernel,
        out_shape=(half, half),
        grid=(width // tile,),
        in_specs=[
            pl.BlockSpec((rows, depth), lambda j: (0, 0)),
            pl.BlockSpec((depth, tile), lambda j: (0, first // tile + j)),
        ],
        out_specs=(spec, spec),
        compiler_params=pltpu.CompilerParams(vmem_limit_bytes=VMEM_LIMIT),
        cost_estimate=pl.CostEstimate(
            flops=16 * rows * depth * width, bytes_accessed=2 * depth * width, transcendentals=0
        ),
        name="head",
    )(normed, weight)


def exponent(value):
    return jnp.floor(jnp.log2(jnp.maximum(value * 1.001, 1e-20))) + 1.0


def encode_kernel(keep, came, coded):
    rows, width = keep.shape
    lanes = lax.broadcasted_iota(jnp.int32, (rows, 128), 1)
    total = keep[...] + came[...]
    high = jnp.max(total, axis=1, keepdims=True)
    low = jnp.min(total, axis=1, keepdims=True)
    middle = 0.5 * high + 0.5 * low
    shift = exponent(jnp.abs(middle))
    unit = jnp.floor(middle * jnp.exp2(15.0 - shift) + 0.5)
    middle = unit * jnp.exp2(shift - 15.0)
    size = exponent(jnp.maximum(high - middle, middle - low))
    scaled = (total - middle) * jnp.exp2(15.0 - size)
    coded[:, :width] = jnp.floor(scaled + 0.5).astype(jnp.int32).astype(jnp.int16)
    info = jnp.where(lanes == 0, unit, jnp.where(lanes == 1, shift, size))
    coded[:, width:] = info.astype(jnp.int32).astype(jnp.int16)


def encode(keep, came, group, count):
    width = keep.shape[1]
    steps = count // ROWS
    source = pl.BlockSpec((ROWS, width), lambda i: (group * steps + i, 0))
    return pl.pallas_call(
        encode_kernel,
        out_shape=jax.ShapeDtypeStruct((count, width + 128), jnp.int16),
        grid=(steps,),
        in_specs=[source, source],
        out_specs=pl.BlockSpec((ROWS, width + 128), lambda i: (i, 0)),
        compiler_params=pltpu.CompilerParams(vmem_limit_bytes=VMEM_LIMIT),
        cost_estimate=COST,
        name="encode",
    )(keep, came)


def row_stats(total, ids):
    top = jnp.max(total, axis=1, keepdims=True)
    sums = jnp.sum(jnp.exp(total - top), axis=1, keepdims=True)
    columns = lax.broadcasted_iota(jnp.int32, total.shape, 1)
    picked = jnp.sum(jnp.where(columns == ids, total, 0.0), axis=1, keepdims=True)
    lanes = lax.broadcasted_iota(jnp.int32, (total.shape[0], 128), 1)
    return jnp.where(lanes == 0, top, jnp.where(lanes == 1, sums, picked))


def finish_chosen_kernel(far, ids, keep, came, *refs):
    total = keep[...] + came[...]
    for wide in refs[:far]:
        total = total + wide[:, : total.shape[1]]
    logits, stats = refs[far:]
    logits[...] = total
    stats[...] = row_stats(total, ids[...])


def finish_others_kernel(far, ids, keep, came, *refs):
    width = keep.shape[1]
    total = keep[...] + came[...]
    for coded in refs[:far]:
        info = coded[:, width:].astype(jnp.int32).astype(F32)
        middle = info[:, :1] * jnp.exp2(info[:, 1:2] - 15.0)
        step = jnp.exp2(info[:, 2:3] - 15.0)
        total = total + (coded[:, :width].astype(jnp.int32).astype(F32) * step + middle)
    refs[far][...] = row_stats(total, ids[...])


def finish_chosen(ids, keep, came, wides, first):
    count, width = ids.shape[0], keep.shape[1]
    own = pl.BlockSpec((count, width), lambda i: (first // count, 0))
    return pl.pallas_call(
        functools.partial(finish_chosen_kernel, len(wides)),
        out_shape=(jax.ShapeDtypeStruct((count, width), F32), jax.ShapeDtypeStruct((count, 128), F32)),
        grid=(1,),
        in_specs=[pl.BlockSpec((count, 1), lambda i: (0, 0)), own, own]
        + [pl.BlockSpec((count, width), lambda i: (0, 0)) for _ in wides],
        out_specs=(
            pl.BlockSpec((count, width), lambda i: (0, 0)),
            pl.BlockSpec((count, 128), lambda i: (0, 0)),
        ),
        cost_estimate=COST,
        name="finish_chosen",
    )(ids, keep, came, *wides)


def finish_others(ids, keep, came, codeds, group):
    count, width = ids.shape[0], keep.shape[1]
    steps = count // ROWS
    own = pl.BlockSpec((ROWS, width), lambda i: (group * steps + i, 0))
    return pl.pallas_call(
        functools.partial(finish_others_kernel, len(codeds)),
        out_shape=jax.ShapeDtypeStruct((count, 128), F32),
        grid=(steps,),
        in_specs=[pl.BlockSpec((ROWS, 1), lambda i: (i, 0)), own, own]
        + [pl.BlockSpec((ROWS, width + 128), lambda i: (i, 0)) for _ in codeds],
        out_specs=pl.BlockSpec((ROWS, 128), lambda i: (i, 0)),
        compiler_params=pltpu.CompilerParams(vmem_limit_bytes=VMEM_LIMIT),
        cost_estimate=COST,
        name="finish_others",
    )(ids, keep, came, *codeds)


def select_kernel(positions, at, drafts, out):
    for r in range(out.shape[1]):
        out[0, pl.ds(r, 1), :] = drafts[pl.ds(r * positions + at[r], 1), :]


def select_drafts(drafts, at, positions, count):
    rows, vocab = drafts.shape
    width = vocab // count
    return pl.pallas_call(
        functools.partial(select_kernel, positions),
        out_shape=jax.ShapeDtypeStruct((count, rows // positions, width), F32),
        grid=(count,),
        in_specs=[
            pl.BlockSpec(memory_space=pltpu.SMEM),
            pl.BlockSpec((rows, width), lambda j: (0, j)),
        ],
        out_specs=pl.BlockSpec((1, rows // positions, width), lambda j: (j, 0, 0)),
        cost_estimate=COST,
        name="select_drafts",
    )(at, drafts)


def shards(n_dp, n_tensor, hidden, gain, head_weight, draft_probs, draft_ids, reject_at):
    tokens, local = hidden.shape
    features = local * n_dp * n_tensor
    depth, width = head_weight.shape
    vocab = width * n_tensor
    requests = reject_at.shape[0]
    owned = draft_ids.shape[0]
    positions = owned // requests
    n_y = n_dp // 2
    nx = 1
    while nx * nx * 4 <= n_tensor:
        nx *= 2
    nz = n_tensor // nx
    d, t = lax.axis_index("dp"), lax.axis_index("tensor")
    y, c = d // 2, d % 2
    z, x = t // nx, t % nx

    mine = requests // n_tensor
    at = lax.dynamic_slice(reject_at, (t * mine,), (mine,))
    drafts = select_drafts(draft_probs, at, positions, n_tensor)

    values = hidden.astype(F32)
    squares = jnp.sum(values * values, axis=1)
    gains = lax.dynamic_update_slice(jnp.zeros((depth,), F32), gain[0].astype(F32), (t * local,))
    small = jnp.concatenate([squares, gains])
    small = jnp.pad(small, (0, -small.shape[0] % 1024)).reshape(-1, 128)
    if n_tensor > 1:
        small = small + lax.ppermute(small, "tensor", [(i, i ^ 1) for i in range(n_tensor)])
    relayed = local % 128 == 0
    if relayed:
        whole = gather_pieces(hidden, nz, nx, small, drafts)
    else:
        whole = {(0, 0): lax.all_gather(hidden, "tensor", axis=1, tiled=True)}
    offsets = list(whole)
    bit = 2
    while bit < n_tensor:
        if relayed and bit == 4:
            small = held_after(small, whole[nz // 2, 0])
        small = small + lax.ppermute(small, "tensor", [(i, i ^ bit) for i in range(n_tensor)])
        bit *= 2
    flat = small.reshape(-1)
    gains = flat[tokens : tokens + depth]

    places = lax.dynamic_update_slice(jnp.zeros((n_dp * requests,), F32), reject_at.astype(F32), (d * requests,))
    small = jnp.concatenate([flat[:tokens], places])
    flat = tree_sum(jnp.pad(small, (0, -small.shape[0] % 1024)).reshape(-1, 128), "dp", n_dp).reshape(-1)
    every_at = flat[tokens : tokens + n_dp * requests].astype(jnp.int32).reshape(n_dp, requests)
    scale = lax.rsqrt(flat[:tokens] / features + EPS)

    turn = []

    def next_turn(value):
        return held_after(value, turn[-1]) if turn else value

    mine = requests // n_tensor
    at = lax.dynamic_slice(reject_at, (t * mine,), (mine,))
    drafts = select_drafts(draft_probs, at, positions, n_tensor)

    rest = owned - requests
    starts = jnp.arange(requests, dtype=jnp.int32) * positions
    steps = jnp.arange(positions - 1, dtype=jnp.int32)

    def chosen_of(at):
        return starts + at

    def others_of(at):
        return (starts[:, None] + steps + (steps >= at[..., None])).reshape(at.shape[:-1] + (rest,))

    owners = jnp.arange(n_dp, dtype=jnp.int32)[:, None]

    hops = [k % n_y for k in range(1, n_y + 1)]
    groups = jnp.stack([((y + k) % n_y) * 2 + core for core in (1 - c, c) for k in hops])
    is_group = (groups[:, None] == jnp.arange(n_dp))[:, :, None]

    def grouped(of_owner):
        return jnp.sum(jnp.where(is_group, of_owner, 0), axis=1).reshape(-1, 1).astype(jnp.int32)

    core_pairs = [(i, i ^ 1) for i in range(n_dp)]

    def y_pairs(k):
        return [(i, ((i // 2 + k) % n_y) * 2 + i % 2) for i in range(n_dp)]

    where = jnp.concatenate([chosen_of(reject_at), others_of(reject_at)])
    ids = jnp.sum(jnp.where(where[:, None] == jnp.arange(owned), draft_ids, 0), axis=1) - t * width
    ids = ids[:, None]

    def span(parts, p):
        quarter = width // sum(parts)
        return sum(parts[:p]) * quarter, parts[p] * quarter

    def do_head(normed, p, parts, tile):
        send, keep = head(next_turn(normed), head_weight, *span(parts, p), tile)
        turn.append(keep)
        return keep, lax.ppermute(send, "dp", core_pairs)

    place = jnp.stack([((z ^ dz) * nx + (x ^ k)) if relayed else 0 * z for dz, k in offsets]).astype(jnp.int32)
    order = jnp.concatenate(
        [grouped(owners * owned + chosen_of(every_at)), grouped(owners * owned + others_of(every_at))]
    )
    chosen_normed, normed = prepare(
        [whole[o] for o in offsets],
        place,
        held_after(order, drafts),
        scale[:, None],
        gains.reshape(-1, local if relayed else depth),
        depth,
        n_dp * requests,
    )
    drafts = held_after(drafts, normed)
    drafts = lax.all_to_all(drafts, "tensor", split_axis=0, concat_axis=0, tiled=True)

    first_heads = [do_head(chosen_normed, p, FIRST_PARTS, TILES[0]) for p in range(len(FIRST_PARTS))]
    chosen_far = []

    def send_chosen(p):
        keep, came = first_heads[p]
        keep = next_turn(keep)
        leaving = [
            keep[n * requests : (n + 1) * requests] + came[n * requests : (n + 1) * requests]
            for n in range(n_y - 1)
        ]
        chosen_far.append([lax.ppermute(v, "dp", y_pairs(k)) for k, v in zip(hops, leaving)])
        turn.extend(leaving[-1:])

    chosen_logits, chosen_stats = [], []

    def do_chosen(p):
        keep, came = first_heads[p]
        part_ids = held_after(next_turn(ids[:requests] - span(FIRST_PARTS, p)[0]), drafts)
        logits, stats = finish_chosen(part_ids, keep, came, chosen_far[p], (n_y - 1) * requests)
        chosen_logits.append(logits)
        chosen_stats.append(stats)
        turn.append(stats)

    for p in range(len(FIRST_PARTS) - 1):
        send_chosen(p)

    rest_heads, coded_far, other_stats = [], [], []

    def send_others(p):
        keep, came = rest_heads[p]
        far = []
        for n, k in enumerate(hops[:-1]):
            coded = encode(next_turn(keep), came, n, rest)
            turn.append(coded)
            far.append(lax.ppermute(coded, "dp", y_pairs(k)))
        coded_far.append(far)

    def do_others(p):
        keep, came = rest_heads[p]
        part_ids = next_turn(ids[requests:] - span(REST_PARTS, p)[0])
        other_stats.append(finish_others(part_ids, keep, came, coded_far[p], n_y - 1))
        turn.append(other_stats[-1])

    for p in range(len(REST_PARTS)):
        rest_heads.append(do_head(normed, p, REST_PARTS, TILES[1]))
        if p == 0:
            send_chosen(len(FIRST_PARTS) - 1)
        else:
            send_others(p - 1)
        if p < len(FIRST_PARTS):
            do_chosen(p)
    send_others(len(REST_PARTS) - 1)
    sent_last = turn[-1]
    for p in range(len(REST_PARTS)):
        do_others(p)

    def joined(stats):
        merged = stats[0][:, :3].T
        for other in stats[1:]:
            merged = merge(merged, other[:, :3].T)
        return merged

    of_chosen = tree_merge(joined(chosen_stats), "tensor", n_tensor)
    chosen_logz = of_chosen[0] + jnp.log(of_chosen[1])
    logits = held_after(jnp.concatenate(chosen_logits, axis=1), sent_last)
    kept = jnp.maximum(jnp.exp(logits - chosen_logz[:, None]) - drafts.reshape(requests, width), 0.0)
    mass = jnp.sum(kept, axis=1)
    zero = jnp.zeros_like(mass)
    of_other = jnp.concatenate([joined(other_stats), jnp.stack([zero, mass, zero])], axis=1)
    of_other = tree_merge(of_other, "tensor", n_tensor)
    mass = of_other[1, rest:]
    of_other = of_other[:, :rest]
    residual = vocab * kept / mass[:, None]
    found = jnp.concatenate(
        [of_chosen[2] - chosen_logz, of_other[2] - (of_other[0] + jnp.log(of_other[1]))]
    )
    token_logprob = jnp.sum(
        jnp.where(where[None, :] == jnp.arange(owned)[:, None], found[None, :], 0.0), axis=1
    )
    return (token_logprob, residual)


def solution(mesh):
    return jax.shard_map(
        functools.partial(shards, mesh.shape["dp"], mesh.shape["tensor"]),
        mesh=mesh,
        in_specs=(
            P(None, ("dp", "tensor")),
            P(None, ("dp", "tensor")),
            P("dp", "tensor"),
            P(("dp", "tensor"), None),
            P("dp"),
            P("dp"),
        ),
        out_specs=(P("dp"), P("dp", "tensor")),
        check_vma=False,
    )
```

```python
import functools

import jax
import jax.numpy as jnp
from jax import lax
from jax.experimental import pallas as pl
from jax.experimental.pallas import tpu as pltpu
from jax.sharding import PartitionSpec as P

EPS = 1e-05
FIRST_PARTS = (2, 2)
REST_PARTS = (2, 1, 1)
ROWS = 32
TILES = 1024, 512
VMEM_LIMIT = 56 * 1024 * 1024
F32 = jnp.float32
COST = pl.CostEstimate(flops=1024, bytes_accessed=1024, transcendentals=0)


def tree_sum(value, axis, count):
    bit = 1
    while bit < count:
        value = value + lax.ppermute(value, axis, [(i, i ^ bit) for i in range(count)])
        bit *= 2
    return value


def merge(first, second):
    top = jnp.maximum(first[0], second[0])
    total = first[1] * jnp.exp(first[0] - top) + second[1] * jnp.exp(second[0] - top)
    return jnp.stack([top, total, first[2] + second[2]])


def tree_merge(stats, axis, count):
    me = lax.axis_index(axis)
    bit = 1
    while bit < count:
        other = lax.ppermute(stats, axis, [(i, i ^ bit) for i in range(count)])
        upper = (me & bit) != 0
        stats = merge(jnp.where(upper, other, stats), jnp.where(upper, stats, other))
        bit *= 2
    return stats


def held_after(value, *earlier):
    if not earlier:
        return value
    return lax.optimization_barrier((value,) + earlier)[0]


def gather_pieces(piece, nz, nx, first):
    count = nz * nx

    def step(value, bits):
        return lax.ppermute(value, "tensor", [(i, i ^ bits) for i in range(count)])

    pieces = {(0, 0): piece}
    bit = nz // 2
    while bit:
        pieces[bit, 0] = step(piece, bit * nx)
        bit //= 2
    for k in range(1, nx):
        pieces[0, k] = step(held_after(piece, first), k)
        pieces[1, k] = step(held_after(pieces[1, 0], pieces[0, k]), k)
    done = [0, 1]
    for offset in range(2, nz):
        near = offset & -offset
        if (offset, 0) not in pieces:
            before = [pieces[o, k] for o in done for k in range(1, nx)]
            pieces[offset, 0] = step(held_after(pieces[offset - near, 0], *before), near * nx)
        for k in range(1, nx):
            ahead = (pieces[offset - 1, k],) if offset > 2 else ()
            pieces[offset, k] = step(held_after(pieces[offset, 0], *ahead), k)
    return pieces


def prepare_kernel(count, place, order, scale, gain, *refs):
    pieces, (chosen, others) = refs[:count], refs[count:]
    first = chosen.shape[0]
    rows, width = pieces[0].shape
    pick = (lax.broadcasted_iota(jnp.int32, (order.shape[0], rows), 1) == order[...]).astype(jnp.bfloat16)
    for n in range(count):
        at = place[n]
        normed = (pieces[n][...].astype(F32) * scale[...] * gain[pl.ds(at, 1), :]).astype(jnp.bfloat16)
        moved = jnp.dot(pick, normed, preferred_element_type=F32).astype(jnp.bfloat16)
        columns = pl.ds(pl.multiple_of(at * width, width), width)
        chosen[:, columns] = moved[:first]
        others[:, columns] = moved[first:]


def prepare(pieces, place, order, scale, gain, depth, first):
    rows = order.shape[0]
    smem = pl.BlockSpec(memory_space=pltpu.SMEM)
    vmem = pl.BlockSpec(memory_space=pltpu.VMEM)
    return pl.pallas_call(
        functools.partial(prepare_kernel, len(pieces)),
        out_shape=(
            jax.ShapeDtypeStruct((first, depth), jnp.bfloat16),
            jax.ShapeDtypeStruct((rows - first, depth), jnp.bfloat16),
        ),
        in_specs=[smem] + [vmem] * (3 + len(pieces)),
        out_specs=(vmem, vmem),
        compiler_params=pltpu.CompilerParams(vmem_limit_bytes=VMEM_LIMIT),
        cost_estimate=COST,
        name="prepare",
    )(place, order, scale, gain, *pieces)


def head_kernel(x, w, send, keep):
    half = send.shape[0]
    out = jnp.dot(x[...], w[...], preferred_element_type=F32)
    send[...] = out[:half]
    keep[...] = out[half:]


def head(normed, weight, first, width, tile):
    rows, depth = normed.shape
    tile = min(tile, width)
    half = jax.ShapeDtypeStruct((rows // 2, width), F32)
    spec = pl.BlockSpec((rows // 2, tile), lambda j: (0, j))
    return pl.pallas_call(
        head_kernel,
        out_shape=(half, half),
        grid=(width // tile,),
        in_specs=[
            pl.BlockSpec((rows, depth), lambda j: (0, 0)),
            pl.BlockSpec((depth, tile), lambda j: (0, first // tile + j)),
        ],
        out_specs=(spec, spec),
        compiler_params=pltpu.CompilerParams(vmem_limit_bytes=VMEM_LIMIT),
        cost_estimate=pl.CostEstimate(
            flops=16 * rows * depth * width, bytes_accessed=2 * depth * width, transcendentals=0
        ),
        name="head",
    )(normed, weight)


def exponent(value):
    return jnp.floor(jnp.log2(jnp.maximum(value * 1.001, 1e-20))) + 1.0


def encode_kernel(keep, came, coded):
    rows, width = keep.shape
    lanes = lax.broadcasted_iota(jnp.int32, (rows, 128), 1)
    total = keep[...] + came[...]
    high = jnp.max(total, axis=1, keepdims=True)
    low = jnp.min(total, axis=1, keepdims=True)
    middle = 0.5 * high + 0.5 * low
    shift = exponent(jnp.abs(middle))
    unit = jnp.floor(middle * jnp.exp2(15.0 - shift) + 0.5)
    middle = unit * jnp.exp2(shift - 15.0)
    size = exponent(jnp.maximum(high - middle, middle - low))
    scaled = (total - middle) * jnp.exp2(15.0 - size)
    coded[:, :width] = jnp.floor(scaled + 0.5).astype(jnp.int32).astype(jnp.int16)
    info = jnp.where(lanes == 0, unit, jnp.where(lanes == 1, shift, size))
    coded[:, width:] = info.astype(jnp.int32).astype(jnp.int16)


def encode(keep, came, group, count):
    width = keep.shape[1]
    steps = count // ROWS
    source = pl.BlockSpec((ROWS, width), lambda i: (group * steps + i, 0))
    return pl.pallas_call(
        encode_kernel,
        out_shape=jax.ShapeDtypeStruct((count, width + 128), jnp.int16),
        grid=(steps,),
        in_specs=[source, source],
        out_specs=pl.BlockSpec((ROWS, width + 128), lambda i: (i, 0)),
        compiler_params=pltpu.CompilerParams(vmem_limit_bytes=VMEM_LIMIT),
        cost_estimate=COST,
        name="encode",
    )(keep, came)


def row_stats(total, ids):
    top = jnp.max(total, axis=1, keepdims=True)
    sums = jnp.sum(jnp.exp(total - top), axis=1, keepdims=True)
    columns = lax.broadcasted_iota(jnp.int32, total.shape, 1)
    picked = jnp.sum(jnp.where(columns == ids, total, 0.0), axis=1, keepdims=True)
    lanes = lax.broadcasted_iota(jnp.int32, (total.shape[0], 128), 1)
    return jnp.where(lanes == 0, top, jnp.where(lanes == 1, sums, picked))


def finish_chosen_kernel(far, ids, keep, came, *refs):
    total = keep[...] + came[...]
    for wide in refs[:far]:
        total = total + wide[:, : total.shape[1]]
    logits, stats = refs[far:]
    logits[...] = total
    stats[...] = row_stats(total, ids[...])


def finish_others_kernel(far, ids, keep, came, *refs):
    width = keep.shape[1]
    total = keep[...] + came[...]
    for coded in refs[:far]:
        info = coded[:, width:].astype(jnp.int32).astype(F32)
        middle = info[:, :1] * jnp.exp2(info[:, 1:2] - 15.0)
        step = jnp.exp2(info[:, 2:3] - 15.0)
        total = total + (coded[:, :width].astype(jnp.int32).astype(F32) * step + middle)
    refs[far][...] = row_stats(total, ids[...])


def finish_chosen(ids, keep, came, wides, first):
    count, width = ids.shape[0], keep.shape[1]
    own = pl.BlockSpec((count, width), lambda i: (first // count, 0))
    return pl.pallas_call(
        functools.partial(finish_chosen_kernel, len(wides)),
        out_shape=(jax.ShapeDtypeStruct((count, width), F32), jax.ShapeDtypeStruct((count, 128), F32)),
        grid=(1,),
        in_specs=[pl.BlockSpec((count, 1), lambda i: (0, 0)), own, own]
        + [pl.BlockSpec((count, width), lambda i: (0, 0)) for _ in wides],
        out_specs=(
            pl.BlockSpec((count, width), lambda i: (0, 0)),
            pl.BlockSpec((count, 128), lambda i: (0, 0)),
        ),
        cost_estimate=COST,
        name="finish_chosen",
    )(ids, keep, came, *wides)


def finish_others(ids, keep, came, codeds, group):
    count, width = ids.shape[0], keep.shape[1]
    steps = count // ROWS
    own = pl.BlockSpec((ROWS, width), lambda i: (group * steps + i, 0))
    return pl.pallas_call(
        functools.partial(finish_others_kernel, len(codeds)),
        out_shape=jax.ShapeDtypeStruct((count, 128), F32),
        grid=(steps,),
        in_specs=[pl.BlockSpec((ROWS, 1), lambda i: (i, 0)), own, own]
        + [pl.BlockSpec((ROWS, width + 128), lambda i: (i, 0)) for _ in codeds],
        out_specs=pl.BlockSpec((ROWS, 128), lambda i: (i, 0)),
        compiler_params=pltpu.CompilerParams(vmem_limit_bytes=VMEM_LIMIT),
        cost_estimate=COST,
        name="finish_others",
    )(ids, keep, came, *codeds)


def select_kernel(positions, at, drafts, out):
    for r in range(out.shape[1]):
        out[0, pl.ds(r, 1), :] = drafts[pl.ds(r * positions + at[r], 1), :]


def select_drafts(drafts, at, positions, count):
    rows, vocab = drafts.shape
    width = vocab // count
    return pl.pallas_call(
        functools.partial(select_kernel, positions),
        out_shape=jax.ShapeDtypeStruct((count, rows // positions, width), F32),
        grid=(count,),
        in_specs=[
            pl.BlockSpec(memory_space=pltpu.SMEM),
            pl.BlockSpec((rows, width), lambda j: (0, j)),
        ],
        out_specs=pl.BlockSpec((1, rows // positions, width), lambda j: (j, 0, 0)),
        cost_estimate=COST,
        name="select_drafts",
    )(at, drafts)


def shards(n_dp, n_tensor, hidden, gain, head_weight, draft_probs, draft_ids, reject_at):
    tokens, local = hidden.shape
    features = local * n_dp * n_tensor
    depth, width = head_weight.shape
    vocab = width * n_tensor
    requests = reject_at.shape[0]
    owned = draft_ids.shape[0]
    positions = owned // requests
    n_y = n_dp // 2
    nx = 1
    while nx * nx * 4 <= n_tensor:
        nx *= 2
    nz = n_tensor // nx
    d, t = lax.axis_index("dp"), lax.axis_index("tensor")
    y, c = d // 2, d % 2
    z, x = t // nx, t % nx

    mine = requests // n_tensor
    at = lax.dynamic_slice(reject_at, (t * mine,), (mine,))
    drafts = select_drafts(draft_probs, at, positions, n_tensor)

    values = hidden.astype(F32)
    squares = jnp.sum(values * values, axis=1)
    gains = lax.dynamic_update_slice(jnp.zeros((depth,), F32), gain[0].astype(F32), (t * local,))
    small = jnp.concatenate([squares, gains])
    small = jnp.pad(small, (0, -small.shape[0] % 1024)).reshape(-1, 128)
    if n_tensor > 1:
        small = small + lax.ppermute(small, "tensor", [(i, i ^ 1) for i in range(n_tensor)])
    relayed = local % 128 == 0
    if relayed:
        whole = gather_pieces(hidden, nz, nx, small)
    else:
        whole = {(0, 0): lax.all_gather(hidden, "tensor", axis=1, tiled=True)}
    offsets = list(whole)
    bit = 2
    while bit < n_tensor:
        if relayed and bit == 4:
            small = held_after(small, whole[nz // 2, 0], drafts)
        small = small + lax.ppermute(small, "tensor", [(i, i ^ bit) for i in range(n_tensor)])
        bit *= 2
    flat = small.reshape(-1)
    gains = flat[tokens : tokens + depth]

    places = lax.dynamic_update_slice(jnp.zeros((n_dp * requests,), F32), reject_at.astype(F32), (d * requests,))
    small = jnp.concatenate([flat[:tokens], places])
    flat = tree_sum(jnp.pad(small, (0, -small.shape[0] % 1024)).reshape(-1, 128), "dp", n_dp).reshape(-1)
    every_at = flat[tokens : tokens + n_dp * requests].astype(jnp.int32).reshape(n_dp, requests)
    scale = lax.rsqrt(flat[:tokens] / features + EPS)

    turn = []

    def next_turn(value):
        return held_after(value, turn[-1]) if turn else value

    mine = requests // n_tensor
    at = lax.dynamic_slice(reject_at, (t * mine,), (mine,))
    drafts = select_drafts(draft_probs, at, positions, n_tensor)

    rest = owned - requests
    starts = jnp.arange(requests, dtype=jnp.int32) * positions
    steps = jnp.arange(positions - 1, dtype=jnp.int32)

    def chosen_of(at):
        return starts + at

    def others_of(at):
        return (starts[:, None] + steps + (steps >= at[..., None])).reshape(at.shape[:-1] + (rest,))

    owners = jnp.arange(n_dp, dtype=jnp.int32)[:, None]

    hops = [k % n_y for k in range(1, n_y + 1)]
    groups = jnp.stack([((y + k) % n_y) * 2 + core for core in (1 - c, c) for k in hops])
    is_group = (groups[:, None] == jnp.arange(n_dp))[:, :, None]

    def grouped(of_owner):
        return jnp.sum(jnp.where(is_group, of_owner, 0), axis=1).reshape(-1, 1).astype(jnp.int32)

    core_pairs = [(i, i ^ 1) for i in range(n_dp)]

    def y_pairs(k):
        return [(i, ((i // 2 + k) % n_y) * 2 + i % 2) for i in range(n_dp)]

    where = jnp.concatenate([chosen_of(reject_at), others_of(reject_at)])
    ids = jnp.sum(jnp.where(where[:, None] == jnp.arange(owned), draft_ids, 0), axis=1) - t * width
    ids = ids[:, None]

    def span(parts, p):
        quarter = width // sum(parts)
        return sum(parts[:p]) * quarter, parts[p] * quarter

    def do_head(normed, p, parts, tile):
        send, keep = head(next_turn(normed), head_weight, *span(parts, p), tile)
        turn.append(keep)
        return keep, lax.ppermute(send, "dp", core_pairs)

    place = jnp.stack([((z ^ dz) * nx + (x ^ k)) if relayed else 0 * z for dz, k in offsets]).astype(jnp.int32)
    order = jnp.concatenate(
        [grouped(owners * owned + chosen_of(every_at)), grouped(owners * owned + others_of(every_at))]
    )
    chosen_normed, normed = prepare(
        [whole[o] for o in offsets],
        place,
        held_after(order, drafts),
        scale[:, None],
        gains.reshape(-1, local if relayed else depth),
        depth,
        n_dp * requests,
    )
    drafts = held_after(drafts, normed)
    drafts = lax.all_to_all(drafts, "tensor", split_axis=0, concat_axis=0, tiled=True)

    first_heads = [do_head(chosen_normed, p, FIRST_PARTS, TILES[0]) for p in range(len(FIRST_PARTS))]
    chosen_far = []

    def send_chosen(p):
        keep, came = first_heads[p]
        keep = next_turn(keep)
        leaving = [
            keep[n * requests : (n + 1) * requests] + came[n * requests : (n + 1) * requests]
            for n in range(n_y - 1)
        ]
        chosen_far.append([lax.ppermute(v, "dp", y_pairs(k)) for k, v in zip(hops, leaving)])
        turn.extend(leaving[-1:])

    chosen_logits, chosen_stats = [], []

    def do_chosen(p):
        keep, came = first_heads[p]
        part_ids = held_after(next_turn(ids[:requests] - span(FIRST_PARTS, p)[0]), drafts)
        logits, stats = finish_chosen(part_ids, keep, came, chosen_far[p], (n_y - 1) * requests)
        chosen_logits.append(logits)
        chosen_stats.append(stats)
        turn.append(stats)

    for p in range(len(FIRST_PARTS) - 1):
        send_chosen(p)

    rest_heads, coded_far, other_stats = [], [], []

    def send_others(p):
        keep, came = rest_heads[p]
        far = []
        for n, k in enumerate(hops[:-1]):
            coded = encode(next_turn(keep), came, n, rest)
            turn.append(coded)
            far.append(lax.ppermute(coded, "dp", y_pairs(k)))
        coded_far.append(far)

    def do_others(p):
        keep, came = rest_heads[p]
        part_ids = next_turn(ids[requests:] - span(REST_PARTS, p)[0])
        other_stats.append(finish_others(part_ids, keep, came, coded_far[p], n_y - 1))
        turn.append(other_stats[-1])

    for p in range(len(REST_PARTS)):
        rest_heads.append(do_head(normed, p, REST_PARTS, TILES[1]))
        if p == 0:
            send_chosen(len(FIRST_PARTS) - 1)
        else:
            send_others(p - 1)
        if p < len(FIRST_PARTS):
            do_chosen(p)
    send_others(len(REST_PARTS) - 1)
    sent_last = turn[-1]
    for p in range(len(REST_PARTS)):
        do_others(p)

    def joined(stats):
        merged = stats[0][:, :3].T
        for other in stats[1:]:
            merged = merge(merged, other[:, :3].T)
        return merged

    of_chosen = tree_merge(joined(chosen_stats), "tensor", n_tensor)
    chosen_logz = of_chosen[0] + jnp.log(of_chosen[1])
    logits = held_after(jnp.concatenate(chosen_logits, axis=1), sent_last)
    kept = jnp.maximum(jnp.exp(logits - chosen_logz[:, None]) - drafts.reshape(requests, width), 0.0)
    mass = jnp.sum(kept, axis=1)
    zero = jnp.zeros_like(mass)
    of_other = jnp.concatenate([joined(other_stats), jnp.stack([zero, mass, zero])], axis=1)
    of_other = tree_merge(of_other, "tensor", n_tensor)
    mass = of_other[1, rest:]
    of_other = of_other[:, :rest]
    residual = vocab * kept / mass[:, None]
    found = jnp.concatenate(
        [of_chosen[2] - chosen_logz, of_other[2] - (of_other[0] + jnp.log(of_other[1]))]
    )
    token_logprob = jnp.sum(
        jnp.where(where[None, :] == jnp.arange(owned)[:, None], found[None, :], 0.0), axis=1
    )
    return (token_logprob, residual)


def solution(mesh):
    return jax.shard_map(
        functools.partial(shards, mesh.shape["dp"], mesh.shape["tensor"]),
        mesh=mesh,
        in_specs=(
            P(None, ("dp", "tensor")),
            P(None, ("dp", "tensor")),
            P("dp", "tensor"),
            P(("dp", "tensor"), None),
            P("dp"),
            P("dp"),
        ),
        out_specs=(P("dp"), P("dp", "tensor")),
        check_vma=False,
    )
```

```python
import functools

import jax
import jax.numpy as jnp
from jax import lax
from jax.experimental import pallas as pl
from jax.experimental.pallas import tpu as pltpu
from jax.sharding import PartitionSpec as P

EPS = 1e-05
FIRST_PARTS = (2, 2)
REST_PARTS = (2, 1, 1)
ROWS = 64
TILES = 1024, 512
VMEM_LIMIT = 56 * 1024 * 1024
F32 = jnp.float32
COST = pl.CostEstimate(flops=1024, bytes_accessed=1024, transcendentals=0)


def tree_sum(value, axis, count):
    bit = 1
    while bit < count:
        value = value + lax.ppermute(value, axis, [(i, i ^ bit) for i in range(count)])
        bit *= 2
    return value


def merge(first, second):
    top = jnp.maximum(first[0], second[0])
    total = first[1] * jnp.exp(first[0] - top) + second[1] * jnp.exp(second[0] - top)
    return jnp.stack([top, total, first[2] + second[2]])


def tree_merge(stats, axis, count):
    me = lax.axis_index(axis)
    bit = 1
    while bit < count:
        other = lax.ppermute(stats, axis, [(i, i ^ bit) for i in range(count)])
        upper = (me & bit) != 0
        stats = merge(jnp.where(upper, other, stats), jnp.where(upper, stats, other))
        bit *= 2
    return stats


def held_after(value, *earlier):
    if not earlier:
        return value
    return lax.optimization_barrier((value,) + earlier)[0]


def gather_pieces(piece, nz, nx, first):
    count = nz * nx

    def step(value, bits):
        return lax.ppermute(value, "tensor", [(i, i ^ bits) for i in range(count)])

    pieces = {(0, 0): piece}
    bit = nz // 2
    while bit:
        pieces[bit, 0] = step(piece, bit * nx)
        bit //= 2
    for k in range(1, nx):
        pieces[0, k] = step(held_after(piece, first), k)
        pieces[1, k] = step(held_after(pieces[1, 0], pieces[0, k]), k)
    done = [0, 1]
    for offset in range(2, nz):
        near = offset & -offset
        if (offset, 0) not in pieces:
            before = [pieces[o, k] for o in done for k in range(1, nx)]
            pieces[offset, 0] = step(held_after(pieces[offset - near, 0], *before), near * nx)
        for k in range(1, nx):
            ahead = (pieces[offset - 1, k],) if offset > 2 else ()
            pieces[offset, k] = step(held_after(pieces[offset, 0], *ahead), k)
    return pieces


def prepare_kernel(count, place, order, scale, gain, *refs):
    pieces, (chosen, others) = refs[:count], refs[count:]
    first = chosen.shape[0]
    rows, width = pieces[0].shape
    pick = (lax.broadcasted_iota(jnp.int32, (order.shape[0], rows), 1) == order[...]).astype(jnp.bfloat16)
    for n in range(count):
        at = place[n]
        normed = (pieces[n][...].astype(F32) * scale[...] * gain[pl.ds(at, 1), :]).astype(jnp.bfloat16)
        moved = jnp.dot(pick, normed, preferred_element_type=F32).astype(jnp.bfloat16)
        columns = pl.ds(pl.multiple_of(at * width, width), width)
        chosen[:, columns] = moved[:first]
        others[:, columns] = moved[first:]


def prepare(pieces, place, order, scale, gain, depth, first):
    rows = order.shape[0]
    smem = pl.BlockSpec(memory_space=pltpu.SMEM)
    vmem = pl.BlockSpec(memory_space=pltpu.VMEM)
    return pl.pallas_call(
        functools.partial(prepare_kernel, len(pieces)),
        out_shape=(
            jax.ShapeDtypeStruct((first, depth), jnp.bfloat16),
            jax.ShapeDtypeStruct((rows - first, depth), jnp.bfloat16),
        ),
        in_specs=[smem] + [vmem] * (3 + len(pieces)),
        out_specs=(vmem, vmem),
        compiler_params=pltpu.CompilerParams(vmem_limit_bytes=VMEM_LIMIT),
        cost_estimate=COST,
        name="prepare",
    )(place, order, scale, gain, *pieces)


def head_kernel(x, w, send, keep):
    half = send.shape[0]
    out = jnp.dot(x[...], w[...], preferred_element_type=F32)
    send[...] = out[:half]
    keep[...] = out[half:]


def head(normed, weight, first, width, tile):
    rows, depth = normed.shape
    tile = min(tile, width)
    half = jax.ShapeDtypeStruct((rows // 2, width), F32)
    spec = pl.BlockSpec((rows // 2, tile), lambda j: (0, j))
    return pl.pallas_call(
        head_kernel,
        out_shape=(half, half),
        grid=(width // tile,),
        in_specs=[
            pl.BlockSpec((rows, depth), lambda j: (0, 0)),
            pl.BlockSpec((depth, tile), lambda j: (0, first // tile + j)),
        ],
        out_specs=(spec, spec),
        compiler_params=pltpu.CompilerParams(vmem_limit_bytes=VMEM_LIMIT),
        cost_estimate=pl.CostEstimate(
            flops=16 * rows * depth * width, bytes_accessed=2 * depth * width, transcendentals=0
        ),
        name="head",
    )(normed, weight)


def exponent(value):
    return jnp.floor(jnp.log2(jnp.maximum(value * 1.001, 1e-20))) + 1.0


def encode_kernel(keep, came, coded):
    rows, width = keep.shape
    lanes = lax.broadcasted_iota(jnp.int32, (rows, 128), 1)
    total = keep[...] + came[...]
    high = jnp.max(total, axis=1, keepdims=True)
    low = jnp.min(total, axis=1, keepdims=True)
    middle = 0.5 * high + 0.5 * low
    shift = exponent(jnp.abs(middle))
    unit = jnp.floor(middle * jnp.exp2(15.0 - shift) + 0.5)
    middle = unit * jnp.exp2(shift - 15.0)
    size = exponent(jnp.maximum(high - middle, middle - low))
    scaled = (total - middle) * jnp.exp2(15.0 - size)
    coded[:, :width] = jnp.floor(scaled + 0.5).astype(jnp.int32).astype(jnp.int16)
    info = jnp.where(lanes == 0, unit, jnp.where(lanes == 1, shift, size))
    coded[:, width:] = info.astype(jnp.int32).astype(jnp.int16)


def encode(keep, came, group, count):
    width = keep.shape[1]
    steps = count // ROWS
    source = pl.BlockSpec((ROWS, width), lambda i: (group * steps + i, 0))
    return pl.pallas_call(
        encode_kernel,
        out_shape=jax.ShapeDtypeStruct((count, width + 128), jnp.int16),
        grid=(steps,),
        in_specs=[source, source],
        out_specs=pl.BlockSpec((ROWS, width + 128), lambda i: (i, 0)),
        compiler_params=pltpu.CompilerParams(vmem_limit_bytes=VMEM_LIMIT),
        cost_estimate=COST,
        name="encode",
    )(keep, came)


def row_stats(total, ids):
    top = jnp.max(total, axis=1, keepdims=True)
    sums = jnp.sum(jnp.exp(total - top), axis=1, keepdims=True)
    columns = lax.broadcasted_iota(jnp.int32, total.shape, 1)
    picked = jnp.sum(jnp.where(columns == ids, total, 0.0), axis=1, keepdims=True)
    lanes = lax.broadcasted_iota(jnp.int32, (total.shape[0], 128), 1)
    return jnp.where(lanes == 0, top, jnp.where(lanes == 1, sums, picked))


def finish_chosen_kernel(far, ids, keep, came, *refs):
    total = keep[...] + came[...]
    for wide in refs[:far]:
        total = total + wide[:, : total.shape[1]]
    logits, stats = refs[far:]
    logits[...] = total
    stats[...] = row_stats(total, ids[...])


def finish_others_kernel(far, ids, keep, came, *refs):
    width = keep.shape[1]
    total = keep[...] + came[...]
    for coded in refs[:far]:
        info = coded[:, width:].astype(jnp.int32).astype(F32)
        middle = info[:, :1] * jnp.exp2(info[:, 1:2] - 15.0)
        step = jnp.exp2(info[:, 2:3] - 15.0)
        total = total + (coded[:, :width].astype(jnp.int32).astype(F32) * step + middle)
    refs[far][...] = row_stats(total, ids[...])


def finish_chosen(ids, keep, came, wides, first):
    count, width = ids.shape[0], keep.shape[1]
    own = pl.BlockSpec((count, width), lambda i: (first // count, 0))
    return pl.pallas_call(
        functools.partial(finish_chosen_kernel, len(wides)),
        out_shape=(jax.ShapeDtypeStruct((count, width), F32), jax.ShapeDtypeStruct((count, 128), F32)),
        grid=(1,),
        in_specs=[pl.BlockSpec((count, 1), lambda i: (0, 0)), own, own]
        + [pl.BlockSpec((count, width), lambda i: (0, 0)) for _ in wides],
        out_specs=(
            pl.BlockSpec((count, width), lambda i: (0, 0)),
            pl.BlockSpec((count, 128), lambda i: (0, 0)),
        ),
        cost_estimate=COST,
        name="finish_chosen",
    )(ids, keep, came, *wides)


def finish_others(ids, keep, came, codeds, group):
    count, width = ids.shape[0], keep.shape[1]
    steps = count // ROWS
    own = pl.BlockSpec((ROWS, width), lambda i: (group * steps + i, 0))
    return pl.pallas_call(
        functools.partial(finish_others_kernel, len(codeds)),
        out_shape=jax.ShapeDtypeStruct((count, 128), F32),
        grid=(steps,),
        in_specs=[pl.BlockSpec((ROWS, 1), lambda i: (i, 0)), own, own]
        + [pl.BlockSpec((ROWS, width + 128), lambda i: (i, 0)) for _ in codeds],
        out_specs=pl.BlockSpec((ROWS, 128), lambda i: (i, 0)),
        compiler_params=pltpu.CompilerParams(vmem_limit_bytes=VMEM_LIMIT),
        cost_estimate=COST,
        name="finish_others",
    )(ids, keep, came, *codeds)


def select_kernel(positions, at, drafts, out):
    for r in range(out.shape[1]):
        out[0, pl.ds(r, 1), :] = drafts[pl.ds(r * positions + at[r], 1), :]


def select_drafts(drafts, at, positions, count):
    rows, vocab = drafts.shape
    width = vocab // count
    return pl.pallas_call(
        functools.partial(select_kernel, positions),
        out_shape=jax.ShapeDtypeStruct((count, rows // positions, width), F32),
        grid=(count,),
        in_specs=[
            pl.BlockSpec(memory_space=pltpu.SMEM),
            pl.BlockSpec((rows, width), lambda j: (0, j)),
        ],
        out_specs=pl.BlockSpec((1, rows // positions, width), lambda j: (j, 0, 0)),
        cost_estimate=COST,
        name="select_drafts",
    )(at, drafts)


def shards(n_dp, n_tensor, hidden, gain, head_weight, draft_probs, draft_ids, reject_at):
    tokens, local = hidden.shape
    features = local * n_dp * n_tensor
    depth, width = head_weight.shape
    vocab = width * n_tensor
    requests = reject_at.shape[0]
    owned = draft_ids.shape[0]
    positions = owned // requests
    n_y = n_dp // 2
    nx = 1
    while nx * nx * 4 <= n_tensor:
        nx *= 2
    nz = n_tensor // nx
    d, t = lax.axis_index("dp"), lax.axis_index("tensor")
    y, c = d // 2, d % 2
    z, x = t // nx, t % nx

    mine = requests // n_tensor
    at = lax.dynamic_slice(reject_at, (t * mine,), (mine,))
    drafts = select_drafts(draft_probs, at, positions, n_tensor)

    values = hidden.astype(F32)
    squares = jnp.sum(values * values, axis=1)
    gains = lax.dynamic_update_slice(jnp.zeros((depth,), F32), gain[0].astype(F32), (t * local,))
    small = jnp.concatenate([squares, gains])
    small = jnp.pad(small, (0, -small.shape[0] % 1024)).reshape(-1, 128)
    if n_tensor > 1:
        small = small + lax.ppermute(small, "tensor", [(i, i ^ 1) for i in range(n_tensor)])
    relayed = local % 128 == 0
    if relayed:
        whole = gather_pieces(hidden, nz, nx, small)
    else:
        whole = {(0, 0): lax.all_gather(hidden, "tensor", axis=1, tiled=True)}
    offsets = list(whole)
    bit = 2
    while bit < n_tensor:
        if relayed and bit == 4:
            small = held_after(small, whole[nz // 2, 0], drafts)
        small = small + lax.ppermute(small, "tensor", [(i, i ^ bit) for i in range(n_tensor)])
        bit *= 2
    flat = small.reshape(-1)
    gains = flat[tokens : tokens + depth]

    places = lax.dynamic_update_slice(jnp.zeros((n_dp * requests,), F32), reject_at.astype(F32), (d * requests,))
    small = jnp.concatenate([flat[:tokens], places])
    flat = tree_sum(jnp.pad(small, (0, -small.shape[0] % 1024)).reshape(-1, 128), "dp", n_dp).reshape(-1)
    every_at = flat[tokens : tokens + n_dp * requests].astype(jnp.int32).reshape(n_dp, requests)
    scale = lax.rsqrt(flat[:tokens] / features + EPS)

    turn = []

    def next_turn(value):
        return held_after(value, turn[-1]) if turn else value

    mine = requests // n_tensor
    at = lax.dynamic_slice(reject_at, (t * mine,), (mine,))
    drafts = select_drafts(draft_probs, at, positions, n_tensor)

    rest = owned - requests
    starts = jnp.arange(requests, dtype=jnp.int32) * positions
    steps = jnp.arange(positions - 1, dtype=jnp.int32)

    def chosen_of(at):
        return starts + at

    def others_of(at):
        return (starts[:, None] + steps + (steps >= at[..., None])).reshape(at.shape[:-1] + (rest,))

    owners = jnp.arange(n_dp, dtype=jnp.int32)[:, None]

    hops = [k % n_y for k in range(1, n_y + 1)]
    groups = jnp.stack([((y + k) % n_y) * 2 + core for core in (1 - c, c) for k in hops])
    is_group = (groups[:, None] == jnp.arange(n_dp))[:, :, None]

    def grouped(of_owner):
        return jnp.sum(jnp.where(is_group, of_owner, 0), axis=1).reshape(-1, 1).astype(jnp.int32)

    core_pairs = [(i, i ^ 1) for i in range(n_dp)]

    def y_pairs(k):
        return [(i, ((i // 2 + k) % n_y) * 2 + i % 2) for i in range(n_dp)]

    where = jnp.concatenate([chosen_of(reject_at), others_of(reject_at)])
    ids = jnp.sum(jnp.where(where[:, None] == jnp.arange(owned), draft_ids, 0), axis=1) - t * width
    ids = ids[:, None]

    def span(parts, p):
        quarter = width // sum(parts)
        return sum(parts[:p]) * quarter, parts[p] * quarter

    def do_head(normed, p, parts, tile):
        send, keep = head(next_turn(normed), head_weight, *span(parts, p), tile)
        turn.append(keep)
        return keep, lax.ppermute(send, "dp", core_pairs)

    place = jnp.stack([((z ^ dz) * nx + (x ^ k)) if relayed else 0 * z for dz, k in offsets]).astype(jnp.int32)
    order = jnp.concatenate(
        [grouped(owners * owned + chosen_of(every_at)), grouped(owners * owned + others_of(every_at))]
    )
    chosen_normed, normed = prepare(
        [whole[o] for o in offsets],
        place,
        held_after(order, drafts),
        scale[:, None],
        gains.reshape(-1, local if relayed else depth),
        depth,
        n_dp * requests,
    )
    drafts = held_after(drafts, normed)
    drafts = lax.all_to_all(drafts, "tensor", split_axis=0, concat_axis=0, tiled=True)

    first_heads = [do_head(chosen_normed, p, FIRST_PARTS, TILES[0]) for p in range(len(FIRST_PARTS))]
    chosen_far = []

    def send_chosen(p):
        keep, came = first_heads[p]
        keep = next_turn(keep)
        leaving = [
            keep[n * requests : (n + 1) * requests] + came[n * requests : (n + 1) * requests]
            for n in range(n_y - 1)
        ]
        chosen_far.append([lax.ppermute(v, "dp", y_pairs(k)) for k, v in zip(hops, leaving)])
        turn.extend(leaving[-1:])

    chosen_logits, chosen_stats = [], []

    def do_chosen(p):
        keep, came = first_heads[p]
        part_ids = held_after(next_turn(ids[:requests] - span(FIRST_PARTS, p)[0]), drafts)
        logits, stats = finish_chosen(part_ids, keep, came, chosen_far[p], (n_y - 1) * requests)
        chosen_logits.append(logits)
        chosen_stats.append(stats)
        turn.append(stats)

    for p in range(len(FIRST_PARTS) - 1):
        send_chosen(p)

    rest_heads, coded_far, other_stats = [], [], []

    def send_others(p):
        keep, came = rest_heads[p]
        far = []
        for n, k in enumerate(hops[:-1]):
            coded = encode(next_turn(keep), came, n, rest)
            turn.append(coded)
            far.append(lax.ppermute(coded, "dp", y_pairs(k)))
        coded_far.append(far)

    def do_others(p):
        keep, came = rest_heads[p]
        part_ids = next_turn(ids[requests:] - span(REST_PARTS, p)[0])
        other_stats.append(finish_others(part_ids, keep, came, coded_far[p], n_y - 1))
        turn.append(other_stats[-1])

    for p in range(len(REST_PARTS)):
        rest_heads.append(do_head(normed, p, REST_PARTS, TILES[1]))
        if p == 0:
            send_chosen(len(FIRST_PARTS) - 1)
        else:
            send_others(p - 1)
        if p < len(FIRST_PARTS):
            do_chosen(p)
    send_others(len(REST_PARTS) - 1)
    sent_last = turn[-1]
    for p in range(len(REST_PARTS)):
        do_others(p)

    def joined(stats):
        merged = stats[0][:, :3].T
        for other in stats[1:]:
            merged = merge(merged, other[:, :3].T)
        return merged

    of_chosen = tree_merge(joined(chosen_stats), "tensor", n_tensor)
    chosen_logz = of_chosen[0] + jnp.log(of_chosen[1])
    logits = held_after(jnp.concatenate(chosen_logits, axis=1), sent_last)
    kept = jnp.maximum(jnp.exp(logits - chosen_logz[:, None]) - drafts.reshape(requests, width), 0.0)
    mass = jnp.sum(kept, axis=1)
    zero = jnp.zeros_like(mass)
    of_other = jnp.concatenate([joined(other_stats), jnp.stack([zero, mass, zero])], axis=1)
    of_other = tree_merge(of_other, "tensor", n_tensor)
    mass = of_other[1, rest:]
    of_other = of_other[:, :rest]
    residual = vocab * kept / mass[:, None]
    found = jnp.concatenate(
        [of_chosen[2] - chosen_logz, of_other[2] - (of_other[0] + jnp.log(of_other[1]))]
    )
    token_logprob = jnp.sum(
        jnp.where(where[None, :] == jnp.arange(owned)[:, None], found[None, :], 0.0), axis=1
    )
    return (token_logprob, residual)


def solution(mesh):
    return jax.shard_map(
        functools.partial(shards, mesh.shape["dp"], mesh.shape["tensor"]),
        mesh=mesh,
        in_specs=(
            P(None, ("dp", "tensor")),
            P(None, ("dp", "tensor")),
            P("dp", "tensor"),
            P(("dp", "tensor"), None),
            P("dp"),
            P("dp"),
        ),
        out_specs=(P("dp"), P("dp", "tensor")),
        check_vma=False,
    )
```
